128 devices in a mesh: rows: 16 (over y_hi, x, core), chan: 8 (over z, y_lo).
Axes of the slice: x: 4, y: 4 (y_hi: 2, y_lo: 2; y = y_hi * 2 + y_lo), z: 4, core: 2. Of those that a mesh axis runs over, the one named last changes fastest.
Arguments:
- activation: bfloat16 [1, 128, 128, 2048], P(None, 'chan', 'rows'), may hold values from -6 to 6
- out_grad: bfloat16 [1, 128, 128, 2048], P(None, 'chan', 'rows'), may hold values from -6 to 6
- weights: bfloat16 [9, 128, 128], replicated, may hold values from -0.1875 to 0.1875
- biases: float32 [128], replicated, may hold values from -3 to 3
Outputs:
- input_grad: bfloat16 [1, 128, 128, 2048], P(None, 'chan', 'rows')
- weight_grad: float32 [9, 128, 128], P(None, 'chan')
- bias_grad: float32 [128], P('chan')
The draws below stay inside these ranges and needn't reach their ends.
All inputs are finite; a program needn't handle non-finite values.
Results may differ from the reference program's by a relative error of at most 0.0075.
Values may be sent and summed in bfloat16 or wider, within the bound.
A program may use at most 64 MiB of HBM per device.

```python
import jax
import jax.numpy as jnp

C = 128
BATCH = 1
MAP_W = 2048
HEIGHT = 128


def level_of(stream_key, shape, shards, low, top_value):
    level, own = 1.0, jax.random.fold_in(stream_key, 6)
    for axis_at, parts in shards:
        heights = jnp.exp(jax.random.uniform(jax.random.fold_in(own, axis_at), (parts,), jnp.float32, low / len(shards), top_value / len(shards)))
        level = level * jnp.repeat(heights, shape[axis_at] // parts).reshape([-1 if axis == axis_at else 1 for axis in range(len(shape))])
    return level


def noise(stream_key, shape, spread, most, shards=(), dtype=jnp.bfloat16):
    gain = level_of(stream_key, shape, shards, -0.22, 0.18) if shards else 1.0
    result = jax.random.normal(stream_key, shape, jnp.float32) * spread * gain
    return jnp.minimum(jnp.maximum(result, -most), most).astype(dtype)


def setup_inputs(seed: int = 0) -> dict:
    keys = jax.random.split(jax.random.key(seed), 5)
    return {
        "activation": noise(keys[0], (BATCH, C, HEIGHT, MAP_W), 1.0, 6.0, ((1, 8), (2, 16))),
        "out_grad": noise(keys[1], (BATCH, C, HEIGHT, MAP_W), 1.0, 6.0, ((1, 8), (2, 16))),
        "weights": noise(keys[2], (9, C, C), (9 * C) ** -0.5, 0.1875),
        "biases": noise(keys[3], (C,), 0.7, 3.0, (), jnp.float32),
    }


def reference(activation, out_grad, weights, biases):
    act = activation.astype(jnp.float32)
    kern = weights.astype(jnp.float32)
    height = act.shape[2]
    extent = act.shape[3]
    act_pad = jnp.pad(act, ((0, 0), (0, 0), (4, 4), (4, 4)))
    pre = jnp.zeros(act.shape, jnp.float32) + biases[None, :, None, None]
    for tap_row in range(3):
        for tap_col in range(3):
            window = act_pad[:, :, 4 * tap_row:4 * tap_row + height, 4 * tap_col:4 * tap_col + extent]
            pre = pre + jnp.einsum('oi,bihw->bohw', kern[3 * tap_row + tap_col], window)
    sig = jax.nn.sigmoid(pre)
    delta = (out_grad.astype(jnp.float32) * sig * (1.0 + pre * (1.0 - sig))).astype(jnp.bfloat16)
    delta_f = delta.astype(jnp.float32)
    delta_pad = jnp.pad(delta_f, ((0, 0), (0, 0), (4, 4), (4, 4)))
    grad_in = jnp.zeros(act.shape, jnp.float32)
    grads = []
    for tap_row in range(3):
        for tap_col in range(3):
            tap = 3 * tap_row + tap_col
            back = delta_pad[:, :, 8 - 4 * tap_row:8 - 4 * tap_row + height, 8 - 4 * tap_col:8 - 4 * tap_col + extent]
            grad_in = grad_in + jnp.einsum('oi,bohw->bihw', kern[tap], back)
            window = act_pad[:, :, 4 * tap_row:4 * tap_row + height, 4 * tap_col:4 * tap_col + extent]
            grads.append(jnp.einsum('bohw,bihw->oi', delta_f, window))
    weight_grad = jnp.stack(grads, axis=0)
    bias_grad = jnp.sum(delta_f, axis=(0, 2, 3))
    return grad_in.astype(jnp.bfloat16), weight_grad, bias_grad
```

```python
import functools

import jax
import jax.numpy as jnp
from jax import lax
from jax.experimental import pallas as pl
from jax.experimental.pallas import tpu as pltpu
from jax.sharding import PartitionSpec as P

MESH = pl.DeviceIdType.MESH
F32 = jnp.float32
BF16 = jnp.bfloat16

CH = 128
OWN = 16
PEERS = 8
COLS = 512
PIECES = 10


def wait_bytes(ref, sem):
    pltpu.make_async_copy(ref, ref, sem).wait()


def column_phases():
    w = lax.broadcasted_iota(jnp.int32, (COLS, COLS), 0)
    m = lax.broadcasted_iota(jnp.int32, (COLS, COLS), 1)
    return jnp.where(w == 4 * (m & 127) + (m >> 7), 1.0, 0.0).astype(BF16)


def split_phases(block, perm, tmp, send):
    for b in range(4):
        x = block[:, :, COLS * b : COLS * (b + 1)].astype(F32).reshape(CH, COLS).astype(BF16)
        y = jnp.dot(x, perm[...], preferred_element_type=F32)
        for phase in range(4):
            tmp[4 * b + phase] = y[:, 128 * phase : 128 * (phase + 1)]
    for b in range(4):
        for phase in range(4):
            for h in range(8):
                f, half, k = h % 2, (h % 4) // 2, h // 4
                rows = tmp[4 * b + phase, pl.ds(h, OWN, stride=8), :]
                send[f, 2 * phase + half, k, :, 128 * b : 128 * (b + 1)] = rows.astype(BF16)


def stack_shifts(src, dst, ahead):
    def body(i, carry):
        at = pl.multiple_of(i * 32, 32)
        x = src[pl.ds(at, 32), :]
        lane = lax.broadcasted_iota(jnp.int32, (32, COLS), 1)
        xf = x.astype(F32)
        later = jnp.where(lane == 0, 0.0, pltpu.roll(xf, 1, 1)).astype(BF16)
        earlier = jnp.where(lane == COLS - 1, 0.0, pltpu.roll(xf, COLS - 1, 1)).astype(BF16)
        first, last = (earlier, later) if ahead else (later, earlier)
        dst[pl.ds(at, 32), :] = first
        dst[pl.ds(at + 128, 32), :] = x
        dst[pl.ds(at + 256, 32), :] = last
        return carry

    lax.fori_loop(0, CH // 32, body, 0)


def kernel(
    ranks,
    act_ref,
    og_ref,
    w_ref,
    bias_ref,
    gin_ref,
    wg_ref,
    bg_ref,
    act_v,
    og_v,
    perm,
    tmp,
    act_s,
    og_s,
    act_a,
    og_a,
    act_x,
    delta_a,
    delta_x,
    w_fwd,
    w_bwd,
    total,
    gin_s,
    gin_r,
    back,
    out_v,
    wg_acc,
    b_acc,
    wg_s,
    wg_r,
    part,
    part_r,
    full,
    load_sem,
    a2a_send,
    a2a_recv,
    halo_send,
    halo_recv,
    ret_send,
    ret_recv,
    wg_send,
    wg_recv,
    part_send,
    part_recv,
    full_send,
    full_recv,
    out_sem,
):
    r = lax.axis_index("rows")
    c = lax.axis_index("chan")
    c16 = pl.multiple_of(c * OWN, OWN)
    dot = functools.partial(jnp.dot, preferred_element_type=F32)

    load_act = pltpu.make_async_copy(act_ref, act_v, load_sem.at[0])
    load_og = pltpu.make_async_copy(og_ref, og_v, load_sem.at[1])
    load_act.start()
    load_og.start()
    for p in range(3):
        for q in range(3):
            pltpu.make_async_copy(
                w_ref.at[3 * p + q],
                w_fwd.at[pl.ds(128 * p, 128), pl.ds(128 * q, 128)],
                load_sem.at[2],
            ).start()

    barrier = pltpu.get_barrier_semaphore()

    def greet_chan(s, carry):
        pl.semaphore_signal(
            barrier, inc=1, device_id={"chan": lax.rem(c + s, PEERS)}, device_id_type=MESH
        )
        return carry

    def greet_rows(s, carry):
        pl.semaphore_signal(
            barrier, inc=1, device_id={"rows": lax.rem(r + s, ranks)}, device_id_type=MESH
        )
        return carry

    lax.fori_loop(1, PEERS, greet_chan, 0)
    lax.fori_loop(1, ranks, greet_rows, 0)

    perm[...] = column_phases()
    load_act.wait()
    split_phases(act_v, perm, tmp, act_s)

    pl.semaphore_wait(barrier, PEERS - 1 + ranks - 1)

    def exchange(kind, f, send, land, rows):
        def step(s, carry):
            to = lax.rem(c + s, PEERS)
            pltpu.make_async_remote_copy(
                src_ref=send.at[f, to],
                dst_ref=land.at[f, rows, pl.ds(c16, OWN), :],
                send_sem=a2a_send.at[2 * kind + f],
                recv_sem=a2a_recv.at[2 * kind + f],
                device_id={"chan": to},
                device_id_type=MESH,
            ).start()
            return carry

        lax.fori_loop(1, PEERS, step, 0)
        pltpu.make_async_copy(
            send.at[f, c], land.at[f, rows, pl.ds(c16, OWN), :], a2a_recv.at[2 * kind + f]
        ).start()

    def halo_copy(buf, kind, f, down):
        at = 2 * (2 * kind + f) + down
        return pltpu.make_async_remote_copy(
            src_ref=buf.at[f, 2 if down else 1],
            dst_ref=buf.at[f, 0 if down else 3],
            send_sem=halo_send.at[at],
            recv_sem=halo_recv.at[at],
            device_id={"rows": lax.rem(r + (1 if down else ranks - 1), ranks)},
            device_id_type=MESH,
        )

    def send_halos(buf, kind, f):
        @pl.when(r < ranks - 1)
        def _():
            halo_copy(buf, kind, f, 1).start()

        @pl.when(r > 0)
        def _():
            halo_copy(buf, kind, f, 0).start()

    def wait_halos(buf, kind, f):
        @pl.when(r > 0)
        def _():
            halo_copy(buf, kind, f, 1).wait_recv()

        @pl.when(r == 0)
        def _():
            buf[f, 0] = jnp.zeros((CH, COLS), BF16)

        @pl.when(r < ranks - 1)
        def _():
            halo_copy(buf, kind, f, 0).wait_recv()

        @pl.when(r == ranks - 1)
        def _():
            buf[f, 3] = jnp.zeros((CH, COLS), BF16)

    own = pl.ds(1, 2)
    both = pl.ds(0, 2)
    exchange(0, 0, act_s, act_a, own)
    load_og.wait()
    split_phases(og_v, perm, tmp, og_s)
    exchange(1, 0, og_s, og_a, both)
    exchange(0, 1, act_s, act_a, own)
    exchange(1, 1, og_s, og_a, both)

    wait_bytes(w_fwd, load_sem.at[2])
    for p in range(3):
        for q in range(3):
            at = (pl.ds(128 * p, 128), pl.ds(128 * q, 128))
            w_bwd[at] = w_fwd[at].astype(F32).T.astype(BF16)
    eye = lax.broadcasted_iota(jnp.int32, (CH, CH), 0) == lax.broadcasted_iota(
        jnp.int32, (CH, CH), 1
    )
    bias = jnp.sum(jnp.where(eye, bias_ref[...], 0.0), axis=1, keepdims=True)
    wg_acc[...] = jnp.zeros_like(wg_acc)
    b_acc[...] = jnp.zeros_like(b_acc)

    def taps_own(w, x, f, order):
        keep, up, down = order
        for n in range(2):
            cols = pl.ds(256 * n, 256)
            first = x[f, 1, :, cols]
            second = x[f, 2, :, cols]
            w_keep = w[128 * keep : 128 * keep + 128, :]
            w_up = w[128 * up : 128 * up + 128, :]
            w_down = w[128 * down : 128 * down + 128, :]
            total[0, :, cols] = dot(w_keep, first) + dot(w_down, second)
            total[1, :, cols] = dot(w_up, first) + dot(w_keep, second)

    def taps_halo(w, x, f, order):
        keep, up, down = order
        for n in range(2):
            cols = pl.ds(256 * n, 256)
            total[0, :, cols] += dot(w[128 * up : 128 * up + 128, :], x[f, 0, :, cols])
            total[1, :, cols] += dot(w[128 * down : 128 * down + 128, :], x[f, 3, :, cols])

    forward = (1, 0, 2)
    backward = (1, 2, 0)

    def start_act(f):
        wait_bytes(act_a.at[f, own], a2a_recv.at[f])
        send_halos(act_a, 0, f)
        for k in (1, 2):
            stack_shifts(act_a.at[f, k], act_x.at[f, k], False)

    def make_delta(f):
        taps_own(w_fwd, act_x, f, forward)
        wait_halos(act_a, 0, f)
        for k in (0, 3):
            stack_shifts(act_a.at[f, k], act_x.at[f, k], False)
        taps_halo(w_fwd, act_x, f, forward)
        wait_bytes(og_a.at[f], a2a_recv.at[2 + f])
        for k in range(2):
            for at in range(0, CH, 16):
                rows = slice(at, at + 16)
                pre = total[k, rows, :] + bias[rows, :]
                s = jax.nn.sigmoid(pre)
                delta = (og_a[f, k, rows, :].astype(F32) * s * (1.0 + pre * (1.0 - s))).astype(BF16)
                delta_a[f, 1 + k, rows, :] = delta
                b_acc[rows, :] += jnp.sum(delta.astype(F32), axis=1, keepdims=True)
        send_halos(delta_a, 1, f)

    def add_weight_grad(f):
        for k in range(2):
            for p in range(3):
                wg_acc[p] += lax.dot_general(
                    delta_a[f, 1 + k],
                    act_x[f, k + p],
                    (((1,), (1,)), ((), ())),
                    preferred_element_type=F32,
                )

    def make_input_grad(f):
        for k in (1, 2):
            stack_shifts(delta_a.at[f, k], delta_x.at[f, k], True)
        taps_own(w_bwd, delta_x, f, backward)
        wait_halos(delta_a, 1, f)
        for k in (0, 3):
            stack_shifts(delta_a.at[f, k], delta_x.at[f, k], True)
        taps_halo(w_bwd, delta_x, f, backward)
        for k in range(2):
            gin_s[f, k] = total[k].astype(BF16)

        def step(s, carry):
            to = lax.rem(c + s, PEERS)
            pltpu.make_async_remote_copy(
                src_ref=gin_s.at[f, :, pl.ds(pl.multiple_of(to * OWN, OWN), OWN), :],
                dst_ref=gin_r.at[f, c],
                send_sem=ret_send.at[f],
                recv_sem=ret_recv.at[f],
                device_id={"chan": to},
                device_id_type=MESH,
            ).start()
            return carry

        lax.fori_loop(1, PEERS, step, 0)
        pltpu.make_async_copy(
            gin_s.at[f, :, pl.ds(c16, OWN), :], gin_r.at[f, c], ret_recv.at[f]
        ).start()

    def send_weight_grad():
        for d in range(PEERS):
            rows = slice(OWN * d, OWN * (d + 1))
            for t in range(9):
                p, q = t // 3, t % 3
                wg_s[d, t] = wg_acc[p, rows, 128 * q : 128 * (q + 1)].astype(BF16)
            wg_s[d, 9] = jnp.broadcast_to(b_acc[rows, :], (OWN, CH)).astype(BF16)

        def step(s, carry):
            to = lax.rem(c + s, PEERS)
            pltpu.make_async_remote_copy(
                src_ref=wg_s.at[to],
                dst_ref=wg_r.at[c],
                send_sem=wg_send,
                recv_sem=wg_recv,
                device_id={"chan": to},
                device_id_type=MESH,
            ).start()
            return carry

        lax.fori_loop(1, PEERS, step, 0)
        pltpu.make_async_copy(wg_s.at[c], wg_r.at[c], wg_recv).start()

    def send_parts():
        wait_bytes(wg_r, wg_recv)
        for t in range(PIECES):
            acc = wg_r[0, t].astype(F32)
            for d in range(1, PEERS):
                acc += wg_r[d, t].astype(F32)
            part[t] = acc
        for t in range(PIECES):
            owner = t % ranks

            @pl.when(r != owner)
            def _():
                pltpu.make_async_remote_copy(
                    src_ref=part.at[t],
                    dst_ref=part_r.at[t, r],
                    send_sem=part_send.at[t],
                    recv_sem=part_recv.at[t],
                    device_id={"rows": owner},
                    device_id_type=MESH,
                ).start()

            @pl.when(r == owner)
            def _():
                pltpu.make_async_copy(part.at[t], part_r.at[t, r], part_recv.at[t]).start()

    def full_copy(t, to):
        return pltpu.make_async_remote_copy(
            src_ref=full.at[t],
            dst_ref=full.at[t],
            send_sem=full_send.at[t],
            recv_sem=full_recv.at[t],
            device_id={"rows": to},
            device_id_type=MESH,
        )

    def send_full():
        for t in range(PIECES):

            @pl.when(r == t % ranks)
            def _():
                wait_bytes(part_r.at[t], part_recv.at[t])
                acc = part_r[t, 0]
                for d in range(1, ranks):
                    acc += part_r[t, d]
                full[t] = acc

                def step(s, carry):
                    full_copy(t, lax.rem(r + s, ranks)).start()
                    return carry

                lax.fori_loop(1, ranks, step, 0)

    def join_phases(f):
        wait_bytes(gin_r.at[f], ret_recv.at[f])
        for b in range(4):
            cols = slice(128 * b, 128 * (b + 1))
            x = jnp.concatenate(
                [
                    jnp.concatenate([gin_r[f, 2 * phase + half, k, :, cols] for phase in range(4)], axis=1)
                    for half in range(2)
                    for k in range(2)
                ],
                axis=0,
            )
            y = lax.dot_general(x, perm[...], (((1,), (1,)), ((), ())), preferred_element_type=F32)
            for half in range(2):
                for k in range(2):
                    h = 4 * k + 2 * half + f
                    at = 16 * (2 * half + k)
                    for n in range(4):
                        back[4 * b + n, OWN * h : OWN * (h + 1), :] = y[
                            at : at + 16, 128 * n : 128 * (n + 1)
                        ]

    def store_input_grad():
        for n in range(16):
            for ch in range(OWN):
                rows = back[n, pl.ds(ch, 8, stride=OWN), :]
                out_v[ch, :, 128 * n : 128 * (n + 1)] = rows.astype(BF16)
        pltpu.make_async_copy(out_v, gin_ref, out_sem.at[0]).start()

    start_act(0)
    make_delta(0)
    start_act(1)
    add_weight_grad(0)
    make_delta(1)
    make_input_grad(0)
    add_weight_grad(1)
    send_weight_grad()
    make_input_grad(1)
    send_parts()
    join_phases(0)
    send_full()
    join_phases(1)
    store_input_grad()

    for t in range(PIECES):

        @pl.when(r != t % ranks)
        def _():
            full_copy(t, r).wait_recv()

    out_w = pltpu.make_async_copy(full.at[pl.ds(0, 9)], wg_ref, out_sem.at[1])
    out_b = pltpu.make_async_copy(full.at[9], bg_ref, out_sem.at[2])
    out_w.start()
    out_b.start()

    for f in range(2):
        wait_bytes(act_s.at[f, pl.ds(0, PEERS - 1)], a2a_send.at[f])
        wait_bytes(og_s.at[f, pl.ds(0, PEERS - 1)], a2a_send.at[2 + f])
        wait_bytes(gin_r.at[f, pl.ds(0, PEERS - 1)], ret_send.at[f])
    wait_bytes(wg_s.at[pl.ds(0, PEERS - 1)], wg_send)
    for kind, buf in ((0, act_a), (1, delta_a)):
        for f in range(2):

            @pl.when(r < ranks - 1)
            def _():
                halo_copy(buf, kind, f, 1).wait_send()

            @pl.when(r > 0)
            def _():
                halo_copy(buf, kind, f, 0).wait_send()

    for t in range(PIECES):

        @pl.when(r != t % ranks)
        def _():
            wait_bytes(part.at[t], part_send.at[t])

        @pl.when(r == t % ranks)
        def _():
            wait_bytes(part_r.at[t, pl.ds(0, ranks - 1)], full_send.at[t])

    pltpu.make_async_copy(out_v, gin_ref, out_sem.at[0]).wait()
    out_w.wait()
    out_b.wait()


def fused(ranks, activation, out_grad, weights, biases):
    height = activation.shape[1]
    extent = activation.shape[2]
    vmem = pltpu.VMEM
    dma = pltpu.SemaphoreType.DMA
    return pl.pallas_call(
        functools.partial(kernel, ranks),
        out_shape=(
            jax.ShapeDtypeStruct((OWN, height, extent), BF16),
            jax.ShapeDtypeStruct((9, OWN, CH), F32),
            jax.ShapeDtypeStruct((OWN, CH), F32),
        ),
        in_specs=[
            pl.BlockSpec(memory_space=pl.ANY),
            pl.BlockSpec(memory_space=pl.ANY),
            pl.BlockSpec(memory_space=pl.ANY),
            pl.BlockSpec(memory_space=pltpu.VMEM),
        ],
        out_specs=[pl.BlockSpec(memory_space=pl.ANY)] * 3,
        scratch_shapes=[
            vmem((OWN, height, extent), BF16),
            vmem((OWN, height, extent), BF16),
            vmem((COLS, COLS), BF16),
            vmem((16, CH, 128), F32),
            vmem((2, PEERS, 2, OWN, COLS), BF16),
            vmem((2, PEERS, 2, OWN, COLS), BF16),
            vmem((2, 4, CH, COLS), BF16),
            vmem((2, 2, CH, COLS), BF16),
            vmem((2, 4, 3 * CH, COLS), BF16),
            vmem((2, 4, CH, COLS), BF16),
            vmem((2, 4, 3 * CH, COLS), BF16),
            vmem((3 * CH, 3 * CH), BF16),
            vmem((3 * CH, 3 * CH), BF16),
            vmem((2, CH, COLS), F32),
            vmem((2, 2, CH, COLS), BF16),
            vmem((2, PEERS, 2, OWN, COLS), BF16),
            vmem((16, CH, 128), F32),
            vmem((OWN, height, extent), BF16),
            vmem((3, CH, 3 * CH), F32),
            vmem((CH, 1), F32),
            vmem((PEERS, PIECES, OWN, CH), BF16),
            vmem((PEERS, PIECES, OWN, CH), BF16),
            vmem((PIECES, OWN, CH), F32),
            vmem((PIECES, ranks, OWN, CH), F32),
            vmem((PIECES, OWN, CH), F32),
            dma((3,)),
            dma((4,)),
            dma((4,)),
            dma((8,)),
            dma((8,)),
            dma((2,)),
            dma((2,)),
            dma,
            dma,
            dma((PIECES,)),
            dma((PIECES,)),
            dma((PIECES,)),
            dma((PIECES,)),
            dma((3,)),
        ],
        compiler_params=pltpu.CompilerParams(
            collective_id=0, has_side_effects=True, vmem_limit_bytes=48 * 1024 * 1024
        ),
        name="conv_backward",
    )(activation, out_grad, weights, biases)


def shards(ranks, activation, out_grad, weights, biases):
    gin, wg, bg = fused(
        ranks, activation[0], out_grad[0], weights, biases.reshape(1, CH)
    )
    return gin[None], wg, bg[:, 0]


def solution(mesh):
    return jax.shard_map(
        functools.partial(shards, mesh.shape["rows"]),
        mesh=mesh,
        in_specs=(P(None, "chan", "rows", None), P(None, "chan", "rows", None), P(), P()),
        out_specs=(P(None, "chan", "rows", None), P(None, "chan", None), P("chan")),
        check_vma=False,
    )
```

```python
import functools

import jax
import jax.numpy as jnp
from jax import lax
from jax.experimental import pallas as pl
from jax.experimental.pallas import tpu as pltpu
from jax.sharding import PartitionSpec as P

MESH = pl.DeviceIdType.MESH
F32 = jnp.float32
BF16 = jnp.bfloat16

CH = 128
OWN = 16
PEERS = 8
COLS = 512
PIECES = 10
HELD = 3


def wait_bytes(ref, sem):
    pltpu.make_async_copy(ref, ref, sem).wait()


def remote(src, dst, send_sem, recv_sem, device):
    return pltpu.make_async_remote_copy(
        src_ref=src,
        dst_ref=dst,
        send_sem=send_sem,
        recv_sem=recv_sem,
        device_id=device,
        device_id_type=MESH,
    )


def local(src, dst, sem):
    return pltpu.make_async_copy(src, dst, sem)


def column_phases():
    w = lax.broadcasted_iota(jnp.int32, (COLS, COLS), 0)
    m = lax.broadcasted_iota(jnp.int32, (COLS, COLS), 1)
    return jnp.where(w == 4 * (m & 127) + (m >> 7), 1.0, 0.0).astype(BF16)


def split_phases(block, perm, tmp, send):
    for b in range(4):
        x = block[:, :, COLS * b : COLS * (b + 1)].astype(F32).reshape(CH, COLS).astype(BF16)
        y = jnp.dot(x, perm[...], preferred_element_type=F32)
        for phase in range(4):
            tmp[4 * b + phase] = y[:, 128 * phase : 128 * (phase + 1)]
    for b in range(4):
        for phase in range(4):
            for h in range(8):
                f, half, k = h % 2, (h % 4) // 2, h // 4
                rows = tmp[4 * b + phase, pl.ds(h, OWN, stride=8), :]
                send[f, 2 * phase + half, k, :, 128 * b : 128 * (b + 1)] = rows.astype(BF16)


def stack_shifts(src, dst, ahead):
    def body(i, carry):
        at = pl.multiple_of(i * 32, 32)
        x = src[pl.ds(at, 32), :]
        lane = lax.broadcasted_iota(jnp.int32, (32, COLS), 1)
        xf = x.astype(F32)
        later = jnp.where(lane == 0, 0.0, pltpu.roll(xf, 1, 1)).astype(BF16)
        earlier = jnp.where(lane == COLS - 1, 0.0, pltpu.roll(xf, COLS - 1, 1)).astype(BF16)
        first, last = (earlier, later) if ahead else (later, earlier)
        dst[pl.ds(at, 32), :] = first
        dst[pl.ds(at + 128, 32), :] = x
        dst[pl.ds(at + 256, 32), :] = last
        return carry

    lax.fori_loop(0, CH // 32, body, 0, unroll=True)


def kernel(
    ranks,
    act_ref,
    og_ref,
    w_ref,
    bias_ref,
    gin_ref,
    wg_ref,
    bg_ref,
    act_v,
    og_v,
    perm,
    tmp,
    act_s,
    og_s,
    act_a,
    og_a,
    act_x,
    delta_a,
    delta_x,
    w_fwd,
    w_bwd,
    total,
    gin_s,
    gin_r,
    back,
    out_v,
    wg_acc,
    b_acc,
    wg_s,
    wg_r,
    part,
    part_r,
    full,
    load_sem,
    a2a_send,
    a2a_recv,
    halo_send,
    halo_recv,
    ret_send,
    ret_recv,
    wg_send,
    wg_recv,
    part_send,
    part_recv,
    out_sem,
):
    r = lax.axis_index("rows")
    c = lax.axis_index("chan")
    c16 = pl.multiple_of(c * OWN, OWN)
    far = r // (ranks // 2)

    xs = ranks // 4
    x = lax.rem(r // 2, xs)

    def first_piece(at):
        return HELD * at - (HELD * xs - PIECES) * (at // (xs - 1))

    def flipped(at):
        return at + 1 - 2 * lax.rem(at, 2)

    def slot_of(at):
        return at + far * (flipped(at) - at)

    dot = functools.partial(jnp.dot, preferred_element_type=F32)

    load_act = pltpu.make_async_copy(act_ref, act_v, load_sem.at[0])
    load_og = pltpu.make_async_copy(og_ref, og_v, load_sem.at[1])
    load_act.start()
    load_og.start()
    for p in range(3):
        for q in range(3):
            pltpu.make_async_copy(
                w_ref.at[3 * p + q],
                w_fwd.at[pl.ds(128 * p, 128), pl.ds(128 * q, 128)],
                load_sem.at[2],
            ).start()

    barrier = pltpu.get_barrier_semaphore()

    def greet_chan(s, carry):
        pl.semaphore_signal(
            barrier, inc=1, device_id={"chan": lax.rem(c + s, PEERS)}, device_id_type=MESH
        )
        return carry

    def greet_rows(s, carry):
        pl.semaphore_signal(
            barrier, inc=1, device_id={"rows": lax.rem(r + s, ranks)}, device_id_type=MESH
        )
        return carry

    lax.fori_loop(1, PEERS, greet_chan, 0)
    lax.fori_loop(1, ranks, greet_rows, 0)
    border = ranks // 2 - 1 + far

    @pl.when(r == border)
    def _():
        pl.semaphore_signal(
            barrier,
            inc=1,
            device_id={"rows": ranks - 1 - border, "chan": flipped(c)},
            device_id_type=MESH,
        )


    perm[...] = column_phases()
    load_act.wait()
    split_phases(act_v, perm, tmp, act_s)

    greeted = PEERS - 1 + ranks - 1

    @pl.when(r == border)
    def _():
        pl.semaphore_wait(barrier, greeted + 1)

    @pl.when(r != border)
    def _():
        pl.semaphore_wait(barrier, greeted)

    def exchange(kind, f, send, land, rows):
        def step(s, carry):
            to = lax.rem(c + s, PEERS)
            remote(send.at[f, slot_of(to)], land.at[f, rows, pl.ds(c16, OWN), :], a2a_send.at[2 * kind + f], a2a_recv.at[2 * kind + f], {"chan": to}).start()
            return carry

        lax.fori_loop(1, PEERS, step, 0)
        local(
            send.at[f, slot_of(c)], land.at[f, rows, pl.ds(c16, OWN), :], a2a_recv.at[2 * kind + f]
        ).start()

    def halo_peer(down):
        to = lax.rem(r + (1 if down else ranks - 1), ranks)
        cross = far + to // (ranks // 2) - 2 * far * (to // (ranks // 2))
        return {"rows": to, "chan": c + cross * (flipped(c) - c)}

    def halo_copy(buf, kind, f, down):
        at = 2 * (2 * kind + f) + down
        return remote(buf.at[f, 2 if down else 1], buf.at[f, 0 if down else 3], halo_send.at[at], halo_recv.at[at], halo_peer(down))

    def send_halos(buf, kind, f):
        @pl.when(r < ranks - 1)
        def _():
            halo_copy(buf, kind, f, 1).start()

        @pl.when(r > 0)
        def _():
            halo_copy(buf, kind, f, 0).start()

    def wait_halos(buf, kind, f):
        @pl.when(r > 0)
        def _():
            halo_copy(buf, kind, f, 1).wait_recv()

        @pl.when(r == 0)
        def _():
            buf[f, 0] = jnp.zeros((CH, COLS), BF16)

        @pl.when(r < ranks - 1)
        def _():
            halo_copy(buf, kind, f, 0).wait_recv()

        @pl.when(r == ranks - 1)
        def _():
            buf[f, 3] = jnp.zeros((CH, COLS), BF16)

    own = pl.ds(1, 2)
    both = pl.ds(0, 2)
    exchange(0, 0, act_s, act_a, own)
    exchange(0, 1, act_s, act_a, own)
    load_og.wait()
    split_phases(og_v, perm, tmp, og_s)
    exchange(1, 0, og_s, og_a, both)
    exchange(1, 1, og_s, og_a, both)

    pltpu.make_async_copy(w_fwd, w_fwd, load_sem.at[2]).wait()
    for p in range(3):
        for q in range(3):
            at = (pl.ds(128 * p, 128), pl.ds(128 * q, 128))
            w_bwd[at] = w_fwd[at].astype(F32).T.astype(BF16)
    eye = lax.broadcasted_iota(jnp.int32, (CH, CH), 0) == lax.broadcasted_iota(
        jnp.int32, (CH, CH), 1
    )
    bias = jnp.sum(jnp.where(eye, bias_ref[...], 0.0), axis=1, keepdims=True)
    wg_acc[...] = jnp.zeros_like(wg_acc)
    b_acc[...] = jnp.zeros_like(b_acc)

    def taps_own(w, x, f, order):
        keep, up, down = order
        for n in range(2):
            cols = pl.ds(256 * n, 256)
            first = x[f, 1, :, cols]
            second = x[f, 2, :, cols]
            w_keep = w[128 * keep : 128 * keep + 128, :]
            w_up = w[128 * up : 128 * up + 128, :]
            w_down = w[128 * down : 128 * down + 128, :]
            total[f, 0, :, cols] = dot(w_keep, first) + dot(w_down, second)
            total[f, 1, :, cols] = dot(w_up, first) + dot(w_keep, second)

    def taps_halo(w, x, f, order):
        keep, up, down = order
        for n in range(2):
            cols = pl.ds(256 * n, 256)
            total[f, 0, :, cols] += dot(w[128 * up : 128 * up + 128, :], x[f, 0, :, cols])
            total[f, 1, :, cols] += dot(w[128 * down : 128 * down + 128, :], x[f, 3, :, cols])

    out_w = pltpu.make_async_copy(full.at[pl.ds(0, 9)], wg_ref, out_sem.at[1])
    out_b = pltpu.make_async_copy(full.at[9], bg_ref, out_sem.at[2])

    forward = (1, 0, 2)
    backward = (1, 2, 0)

    def start_act(f):
        wait_bytes(act_a.at[f, own], a2a_recv.at[f])
        send_halos(act_a, 0, f)
        for k in (1, 2):
            stack_shifts(act_a.at[f, k], act_x.at[f, k], False)

        taps_own(w_fwd, act_x, f, forward)

    def finish_pre(f):
        wait_halos(act_a, 0, f)
        for k in (0, 3):
            stack_shifts(act_a.at[f, k], act_x.at[f, k], False)
        taps_halo(w_fwd, act_x, f, forward)

    def make_delta(f):
        wait_bytes(og_a.at[f], a2a_recv.at[2 + f])
        for k in range(2):
            for at in range(0, CH, 16):
                rows = slice(at, at + 16)
                pre = total[f, k, rows, :] + bias[rows, :]
                s = jax.nn.sigmoid(pre)
                delta = (og_a[f, k, rows, :].astype(F32) * s * (1.0 + pre * (1.0 - s))).astype(BF16)
                delta_a[f, 1 + k, rows, :] = delta
                b_acc[rows, :] += jnp.sum(delta.astype(F32), axis=1, keepdims=True)
        send_halos(delta_a, 1, f)

    def add_weight_grad(f):
        for k in range(2):
            for p in range(3):
                wg_acc[p] += lax.dot_general(
                    delta_a[f, 1 + k],
                    act_x[f, k + p],
                    (((1,), (1,)), ((), ())),
                    preferred_element_type=F32,
                )

    def start_input_grad(f):
        for k in (1, 2):
            stack_shifts(delta_a.at[f, k], delta_x.at[f, k], True)
        taps_own(w_bwd, delta_x, f, backward)

    def make_input_grad(f):
        wait_halos(delta_a, 1, f)
        for k in (0, 3):
            stack_shifts(delta_a.at[f, k], delta_x.at[f, k], True)
        taps_halo(w_bwd, delta_x, f, backward)
        for k in range(2):
            gin_s[f, k] = total[f, k].astype(BF16)

        def step(s, carry):
            to = lax.rem(c + s, PEERS)
            remote(gin_s.at[f, :, pl.ds(pl.multiple_of(to * OWN, OWN), OWN), :], gin_r.at[f, slot_of(c)], ret_send.at[f], ret_recv.at[f], {"chan": to}).start()
            return carry

        lax.fori_loop(1, PEERS, step, 0)
        local(
            gin_s.at[f, :, pl.ds(c16, OWN), :], gin_r.at[f, slot_of(c)], ret_recv.at[f]
        ).start()

    def send_weight_grad():
        for d in range(PEERS):
            rows = slice(OWN * d, OWN * (d + 1))
            for t in range(9):
                p, q = t // 3, t % 3
                wg_s[d, t] = wg_acc[p, rows, 128 * q : 128 * (q + 1)].astype(BF16)
            wg_s[d, 9] = jnp.broadcast_to(b_acc[rows, :], (OWN, CH)).astype(BF16)

        def piece_copy(x_to, to):
            return remote(
                wg_s.at[to, pl.ds(first_piece(x_to), HELD)],
                wg_r.at[x * PEERS + c],
                wg_send,
                wg_recv,
                {"rows": r + 2 * (x_to - x), "chan": to},
            )

        for dx in range(xs):
            x_to = lax.rem(x + dx, xs)

            def step(s, carry):
                piece_copy(x_to, lax.rem(c + s, PEERS)).start()
                return carry

            lax.fori_loop(1 if dx == 0 else 0, PEERS, step, 0)
        local(wg_s.at[c, pl.ds(first_piece(x), HELD)], wg_r.at[x * PEERS + c], wg_recv).start()

    def send_parts():
        wait_bytes(wg_r, wg_recv)
        for t in range(HELD):
            acc = wg_r[0, t].astype(F32)
            for d in range(1, xs * PEERS):
                acc += wg_r[d, t].astype(F32)
            part[t] = acc.astype(BF16)

        def step(s, carry):
            remote(
                part, part_r.at[r], part_send, part_recv, {"rows": lax.rem(r + s, ranks)}
            ).start()
            return carry

        lax.fori_loop(1, ranks, step, 0)
        local(part, part_r.at[r], part_recv).start()

    def finish_weight_grad():
        wait_bytes(part_r, part_recv)
        for t in range(PIECES):
            x_of = min(t // HELD, xs - 1)
            at = t - first_piece(x_of)
            held = [
                part_r[2 * (xs * half + x_of) + core, at].astype(F32)
                for half in range(2)
                for core in range(2)
            ]
            full[t] = (held[0] + held[1]) + (held[2] + held[3])
        out_w.start()
        out_b.start()

    def join_phases(f):
        wait_bytes(gin_r.at[f], ret_recv.at[f])
        for b in range(4):
            cols = slice(128 * b, 128 * (b + 1))
            x = jnp.concatenate(
                [
                    jnp.concatenate([gin_r[f, 2 * phase + half, k, :, cols] for phase in range(4)], axis=1)
                    for half in range(2)
                    for k in range(2)
                ],
                axis=0,
            )
            y = lax.dot_general(x, perm[...], (((1,), (1,)), ((), ())), preferred_element_type=F32)
            for half in range(2):
                for k in range(2):
                    h = 4 * k + 2 * half + f
                    at = 16 * (2 * half + k)
                    for n in range(4):
                        back[4 * b + n, OWN * h : OWN * (h + 1), :] = y[
                            at : at + 16, 128 * n : 128 * (n + 1)
                        ]

    def store_input_grad():
        for n in range(16):
            for ch in range(OWN):
                rows = back[n, pl.ds(ch, 8, stride=OWN), :]
                out_v[ch, :, 128 * n : 128 * (n + 1)] = rows.astype(BF16)
        pltpu.make_async_copy(out_v, gin_ref, out_sem.at[0]).start()

    start_act(0)
    start_act(1)
    finish_pre(0)
    make_delta(0)
    finish_pre(1)
    add_weight_grad(0)
    start_input_grad(0)
    make_delta(1)
    add_weight_grad(1)
    send_weight_grad()
    make_input_grad(0)
    start_input_grad(1)
    make_input_grad(1)
    send_parts()
    join_phases(0)
    join_phases(1)
    store_input_grad()
    finish_weight_grad()

    for f in range(2):
        wait_bytes(act_s.at[f, pl.ds(0, PEERS - 1)], a2a_send.at[f])
        wait_bytes(og_s.at[f, pl.ds(0, PEERS - 1)], a2a_send.at[2 + f])
        wait_bytes(gin_r.at[f, pl.ds(0, PEERS - 1)], ret_send.at[f])
    wait_bytes(wg_r.at[pl.ds(0, xs * PEERS - 1)], wg_send)
    wait_bytes(part_r.at[pl.ds(0, ranks - 1)], part_send)
    for kind, buf in ((0, act_a), (1, delta_a)):
        for f in range(2):

            @pl.when(r < ranks - 1)
            def _():
                halo_copy(buf, kind, f, 1).wait_send()

            @pl.when(r > 0)
            def _():
                halo_copy(buf, kind, f, 0).wait_send()

    pltpu.make_async_copy(out_v, gin_ref, out_sem.at[0]).wait()
    out_w.wait()
    out_b.wait()


def fused(ranks, activation, out_grad, weights, biases):
    height = activation.shape[1]
    extent = activation.shape[2]
    vmem = pltpu.VMEM
    dma = pltpu.SemaphoreType.DMA
    return pl.pallas_call(
        functools.partial(kernel, ranks),
        out_shape=(
            jax.ShapeDtypeStruct((OWN, height, extent), BF16),
            jax.ShapeDtypeStruct((9, OWN, CH), F32),
            jax.ShapeDtypeStruct((OWN, CH), F32),
        ),
        in_specs=[
            pl.BlockSpec(memory_space=pl.ANY),
            pl.BlockSpec(memory_space=pl.ANY),
            pl.BlockSpec(memory_space=pl.ANY),
            pl.BlockSpec(memory_space=pltpu.VMEM),
        ],
        out_specs=[pl.BlockSpec(memory_space=pl.ANY)] * 3,
        scratch_shapes=[
            vmem((OWN, height, extent), BF16),
            vmem((OWN, height, extent), BF16),
            vmem((COLS, COLS), BF16),
            vmem((16, CH, 128), F32),
            vmem((2, PEERS, 2, OWN, COLS), BF16),
            vmem((2, PEERS, 2, OWN, COLS), BF16),
            vmem((2, 4, CH, COLS), BF16),
            vmem((2, 2, CH, COLS), BF16),
            vmem((2, 4, 3 * CH, COLS), BF16),
            vmem((2, 4, CH, COLS), BF16),
            vmem((2, 4, 3 * CH, COLS), BF16),
            vmem((3 * CH, 3 * CH), BF16),
            vmem((3 * CH, 3 * CH), BF16),
            vmem((2, 2, CH, COLS), F32),
            vmem((2, 2, CH, COLS), BF16),
            vmem((2, PEERS, 2, OWN, COLS), BF16),
            vmem((16, CH, 128), F32),
            vmem((OWN, height, extent), BF16),
            vmem((3, CH, 3 * CH), F32),
            vmem((CH, 1), F32),
            vmem((PEERS, PIECES, OWN, CH), BF16),
            vmem((ranks // 4 * PEERS, HELD, OWN, CH), BF16),
            vmem((HELD, OWN, CH), BF16),
            vmem((ranks, HELD, OWN, CH), BF16),
            vmem((PIECES, OWN, CH), F32),
            dma((3,)),
            dma((4,)),
            dma((4,)),
            dma((8,)),
            dma((8,)),
            dma((2,)),
            dma((2,)),
            dma,
            dma,
            dma,
            dma,
            dma((3,)),
        ],
        compiler_params=pltpu.CompilerParams(
            collective_id=0, has_side_effects=True, vmem_limit_bytes=60 * 1024 * 1024
        ),
        name="conv_backward",
    )(activation, out_grad, weights, biases)


def shards(ranks, activation, out_grad, weights, biases):
    gin, wg, bg = fused(
        ranks, activation[0], out_grad[0], weights, biases.reshape(1, CH)
    )
    return gin[None], wg, bg[:, 0]


def solution(mesh):
    return jax.shard_map(
        functools.partial(shards, mesh.shape["rows"]),
        mesh=mesh,
        in_specs=(P(None, "chan", "rows", None), P(None, "chan", "rows", None), P(), P()),
        out_specs=(P(None, "chan", "rows", None), P(None, "chan", None), P("chan")),
        check_vma=False,
    )
```

```python
import functools

import jax
import jax.numpy as jnp
from jax import lax
from jax.experimental import pallas as pl
from jax.experimental.pallas import tpu as pltpu
from jax.sharding import PartitionSpec as P

MESH = pl.DeviceIdType.MESH
F32 = jnp.float32
BF16 = jnp.bfloat16

CH = 128
OWN = 16
PEERS = 8
COLS = 512
PIECES = 10
HELD = 3


def wait_bytes(ref, sem):
    pltpu.make_async_copy(ref, ref, sem).wait()


def remote(src, dst, send_sem, recv_sem, device):
    return pltpu.make_async_remote_copy(
        src_ref=src,
        dst_ref=dst,
        send_sem=send_sem,
        recv_sem=recv_sem,
        device_id=device,
        device_id_type=MESH,
    )


def local(src, dst, sem):
    return pltpu.make_async_copy(src, dst, sem)


def column_phases():
    w = lax.broadcasted_iota(jnp.int32, (COLS, COLS), 0)
    m = lax.broadcasted_iota(jnp.int32, (COLS, COLS), 1)
    return jnp.where(w == 4 * (m & 127) + (m >> 7), 1.0, 0.0).astype(BF16)


def split_phases(block, perm, tmp, send):
    for b in range(4):
        x = block[:, :, COLS * b : COLS * (b + 1)].astype(F32).reshape(CH, COLS).astype(BF16)
        y = jnp.dot(x, perm[...], preferred_element_type=F32)
        for phase in range(4):
            tmp[4 * b + phase] = y[:, 128 * phase : 128 * (phase + 1)]
    for b in range(4):
        for phase in range(4):
            for h in range(8):
                f, half, k = h % 2, (h % 4) // 2, h // 4
                rows = tmp[4 * b + phase, pl.ds(h, OWN, stride=8), :]
                send[f, 2 * phase + half, k, :, 128 * b : 128 * (b + 1)] = rows.astype(BF16)


def stack_shifts(src, dst, ahead):
    def body(i, carry):
        at = pl.multiple_of(i * 32, 32)
        x = src[pl.ds(at, 32), :]
        lane = lax.broadcasted_iota(jnp.int32, (32, COLS), 1)
        xf = x.astype(F32)
        later = jnp.where(lane == 0, 0.0, pltpu.roll(xf, 1, 1)).astype(BF16)
        earlier = jnp.where(lane == COLS - 1, 0.0, pltpu.roll(xf, COLS - 1, 1)).astype(BF16)
        first, last = (earlier, later) if ahead else (later, earlier)
        dst[pl.ds(at, 32), :] = first
        dst[pl.ds(at + 128, 32), :] = x
        dst[pl.ds(at + 256, 32), :] = last
        return carry

    lax.fori_loop(0, CH // 32, body, 0, unroll=True)


def kernel(
    ranks,
    act_ref,
    og_ref,
    w_ref,
    bias_ref,
    gin_r,
    part_r,
    act_v,
    og_v,
    perm,
    tmp,
    act_s,
    og_s,
    act_a,
    og_a,
    act_x,
    delta_a,
    delta_x,
    w_fwd,
    w_bwd,
    total,
    gin_s,
    wg_acc,
    b_acc,
    wg_s,
    wg_r,
    part,
    ring_sem,
    load_sem,
    a2a_send,
    a2a_recv,
    halo_send,
    halo_recv,
    ret_send,
    ret_recv,
    wg_send,
    wg_recv,
    part_send,
    part_recv,
):
    r = lax.axis_index("rows")
    c = lax.axis_index("chan")
    c16 = pl.multiple_of(c * OWN, OWN)
    far = r // (ranks // 2)

    xs = ranks // 4
    x = lax.rem(r // 2, xs)

    def first_piece(at):
        return HELD * at - (HELD * xs - PIECES) * (at // (xs - 1))

    def flipped(at):
        return at + 1 - 2 * lax.rem(at, 2)

    def slot_of(at):
        return at + far * (flipped(at) - at)

    dot = functools.partial(jnp.dot, preferred_element_type=F32)

    load_act = pltpu.make_async_copy(act_ref, act_v, load_sem.at[0])
    load_og = pltpu.make_async_copy(og_ref, og_v, load_sem.at[1])
    load_act.start()
    load_og.start()
    for p in range(3):
        for q in range(3):
            pltpu.make_async_copy(
                w_ref.at[3 * p + q],
                w_fwd.at[pl.ds(128 * p, 128), pl.ds(128 * q, 128)],
                load_sem.at[2],
            ).start()

    barrier = pltpu.get_barrier_semaphore()

    def greet_chan(s, carry):
        pl.semaphore_signal(
            barrier, inc=1, device_id={"chan": lax.rem(c + s, PEERS)}, device_id_type=MESH
        )
        return carry

    lax.fori_loop(1, PEERS, greet_chan, 0)

    def ring_peer(step):
        to = lax.rem(r + step + ranks, ranks)
        its = to // (ranks // 2)
        cross = far + its - 2 * far * its
        return {"rows": to, "chan": c + cross * (flipped(c) - c)}

    for step in (1, -1):
        pl.semaphore_signal(barrier, inc=1, device_id=ring_peer(step), device_id_type=MESH)

    def tell(n):
        for step in (2**n, -(2**n))[: 1 if 2 ** (n + 1) == ranks else 2]:
            pl.semaphore_signal(
                ring_sem.at[n], inc=1, device_id=ring_peer(step), device_id_type=MESH
            )

    def hear(n):
        pl.semaphore_wait(ring_sem.at[n], 1 if 2 ** (n + 1) == ranks else 2)

    perm[...] = column_phases()
    load_act.wait()
    split_phases(act_v, perm, tmp, act_s)

    pl.semaphore_wait(barrier, PEERS - 1 + 2)

    def exchange(kind, f, send, land, rows):
        def step(s, carry):
            to = lax.rem(c + s, PEERS)
            remote(send.at[f, slot_of(to)], land.at[f, rows, pl.ds(c16, OWN), :], a2a_send.at[2 * kind + f], a2a_recv.at[2 * kind + f], {"chan": to}).start()
            return carry

        lax.fori_loop(1, PEERS, step, 0)
        local(
            send.at[f, slot_of(c)], land.at[f, rows, pl.ds(c16, OWN), :], a2a_recv.at[2 * kind + f]
        ).start()

    def halo_copy(buf, kind, f, down):
        at = 2 * (2 * kind + f) + down
        return remote(buf.at[f, 2 if down else 1], buf.at[f, 0 if down else 3], halo_send.at[at], halo_recv.at[at], ring_peer(1 if down else -1))

    def send_halos(buf, kind, f):
        @pl.when(r < ranks - 1)
        def _():
            halo_copy(buf, kind, f, 1).start()

        @pl.when(r > 0)
        def _():
            halo_copy(buf, kind, f, 0).start()

    def wait_halos(buf, kind, f):
        @pl.when(r > 0)
        def _():
            halo_copy(buf, kind, f, 1).wait_recv()

        @pl.when(r == 0)
        def _():
            buf[f, 0] = jnp.zeros((CH, COLS), BF16)

        @pl.when(r < ranks - 1)
        def _():
            halo_copy(buf, kind, f, 0).wait_recv()

        @pl.when(r == ranks - 1)
        def _():
            buf[f, 3] = jnp.zeros((CH, COLS), BF16)

    own = pl.ds(1, 2)
    both = pl.ds(0, 2)
    exchange(0, 0, act_s, act_a, own)
    exchange(0, 1, act_s, act_a, own)
    tell(0)
    load_og.wait()
    split_phases(og_v, perm, tmp, og_s)
    exchange(1, 0, og_s, og_a, both)
    exchange(1, 1, og_s, og_a, both)

    pltpu.make_async_copy(w_fwd, w_fwd, load_sem.at[2]).wait()
    for p in range(3):
        for q in range(3):
            at = (pl.ds(128 * p, 128), pl.ds(128 * q, 128))
            w_bwd[at] = w_fwd[at].astype(F32).T.astype(BF16)
    eye = lax.broadcasted_iota(jnp.int32, (CH, CH), 0) == lax.broadcasted_iota(
        jnp.int32, (CH, CH), 1
    )
    bias = jnp.sum(jnp.where(eye, bias_ref[...], 0.0), axis=1, keepdims=True)
    hear(0)
    tell(1)
    wg_acc[...] = jnp.zeros_like(wg_acc)
    b_acc[...] = jnp.zeros_like(b_acc)

    def taps_own(w, x, f, order):
        keep, up, down = order
        for n in range(2):
            cols = pl.ds(256 * n, 256)
            first = x[f, 1, :, cols]
            second = x[f, 2, :, cols]
            w_keep = w[128 * keep : 128 * keep + 128, :]
            w_up = w[128 * up : 128 * up + 128, :]
            w_down = w[128 * down : 128 * down + 128, :]
            total[f, 0, :, cols] = dot(w_keep, first) + dot(w_down, second)
            total[f, 1, :, cols] = dot(w_up, first) + dot(w_keep, second)

    def taps_halo(w, x, f, order):
        keep, up, down = order
        for n in range(2):
            cols = pl.ds(256 * n, 256)
            total[f, 0, :, cols] += dot(w[128 * up : 128 * up + 128, :], x[f, 0, :, cols])
            total[f, 1, :, cols] += dot(w[128 * down : 128 * down + 128, :], x[f, 3, :, cols])

    forward = (1, 0, 2)
    backward = (1, 2, 0)

    def start_act(f):
        wait_bytes(act_a.at[f, own], a2a_recv.at[f])
        send_halos(act_a, 0, f)
        for k in (1, 2):
            stack_shifts(act_a.at[f, k], act_x.at[f, k], False)

        taps_own(w_fwd, act_x, f, forward)

    def finish_pre(f):
        wait_halos(act_a, 0, f)
        for k in (0, 3):
            stack_shifts(act_a.at[f, k], act_x.at[f, k], False)
        taps_halo(w_fwd, act_x, f, forward)

    def make_delta(f):
        wait_bytes(og_a.at[f], a2a_recv.at[2 + f])
        for k in range(2):
            for at in range(0, CH, 16):
                rows = slice(at, at + 16)
                pre = total[f, k, rows, :] + bias[rows, :]
                s = jax.nn.sigmoid(pre)
                delta = (og_a[f, k, rows, :].astype(F32) * s * (1.0 + pre * (1.0 - s))).astype(BF16)
                delta_a[f, 1 + k, rows, :] = delta
                b_acc[rows, :] += jnp.sum(delta.astype(F32), axis=1, keepdims=True)
        send_halos(delta_a, 1, f)

    def add_weight_grad(f):
        for k in range(2):
            for p in range(3):
                wg_acc[p] += lax.dot_general(
                    delta_a[f, 1 + k],
                    act_x[f, k + p],
                    (((1,), (1,)), ((), ())),
                    preferred_element_type=F32,
                )

    def start_input_grad(f):
        for k in (1, 2):
            stack_shifts(delta_a.at[f, k], delta_x.at[f, k], True)
        taps_own(w_bwd, delta_x, f, backward)

    def make_input_grad(f):
        wait_halos(delta_a, 1, f)
        for k in (0, 3):
            stack_shifts(delta_a.at[f, k], delta_x.at[f, k], True)
        taps_halo(w_bwd, delta_x, f, backward)
        for k in range(2):
            gin_s[f, k] = total[f, k].astype(BF16)

        def step(s, carry):
            to = lax.rem(c + s, PEERS)
            remote(gin_s.at[f, :, pl.ds(pl.multiple_of(to * OWN, OWN), OWN), :], gin_r.at[f, slot_of(c)], ret_send.at[f], ret_recv.at[f], {"chan": to}).start()
            return carry

        lax.fori_loop(1, PEERS, step, 0)
        local(
            gin_s.at[f, :, pl.ds(c16, OWN), :], gin_r.at[f, slot_of(c)], ret_recv.at[f]
        ).start()

    def send_weight_grad():
        for d in range(PEERS):
            rows = slice(OWN * d, OWN * (d + 1))
            for t in range(9):
                p, q = t // 3, t % 3
                wg_s[d, t] = wg_acc[p, rows, 128 * q : 128 * (q + 1)].astype(BF16)
            wg_s[d, 9] = jnp.broadcast_to(b_acc[rows, :], (OWN, CH)).astype(BF16)

        def piece_copy(x_to, to):
            return remote(
                wg_s.at[to, pl.ds(first_piece(x_to), HELD)],
                wg_r.at[x * PEERS + c],
                wg_send,
                wg_recv,
                {"rows": r + 2 * (x_to - x), "chan": to},
            )

        for dx in range(xs):
            x_to = lax.rem(x + dx, xs)

            def step(s, carry):
                piece_copy(x_to, lax.rem(c + s, PEERS)).start()
                return carry

            lax.fori_loop(1 if dx == 0 else 0, PEERS, step, 0)
        local(wg_s.at[c, pl.ds(first_piece(x), HELD)], wg_r.at[x * PEERS + c], wg_recv).start()

    def send_parts():
        wait_bytes(wg_r, wg_recv)
        for t in range(HELD):
            acc = wg_r[0, t].astype(F32)
            for d in range(1, xs * PEERS):
                acc += wg_r[d, t].astype(F32)
            part[t] = acc.astype(BF16)

        def step(s, carry):
            remote(
                part, part_r.at[r], part_send, part_recv, {"rows": lax.rem(r + s, ranks)}
            ).start()
            return carry

        lax.fori_loop(1, ranks, step, 0)
        local(part, part_r.at[r], part_recv).start()

    start_act(0)
    hear(1)
    tell(2)
    start_act(1)
    hear(2)
    tell(3)
    finish_pre(0)
    make_delta(0)
    finish_pre(1)
    add_weight_grad(0)
    start_input_grad(0)
    hear(3)
    make_delta(1)
    add_weight_grad(1)
    send_weight_grad()
    make_input_grad(0)
    start_input_grad(1)
    make_input_grad(1)
    send_parts()
    for f in range(2):
        wait_bytes(gin_r.at[f], ret_recv.at[f])
    wait_bytes(part_r, part_recv)

    for f in range(2):
        wait_bytes(act_s.at[f, pl.ds(0, PEERS - 1)], a2a_send.at[f])
        wait_bytes(og_s.at[f, pl.ds(0, PEERS - 1)], a2a_send.at[2 + f])
        wait_bytes(gin_r.at[f, pl.ds(0, PEERS - 1)], ret_send.at[f])
    wait_bytes(wg_r.at[pl.ds(0, xs * PEERS - 1)], wg_send)
    wait_bytes(part_r.at[pl.ds(0, ranks - 1)], part_send)
    for kind, buf in ((0, act_a), (1, delta_a)):
        for f in range(2):

            @pl.when(r < ranks - 1)
            def _():
                halo_copy(buf, kind, f, 1).wait_send()

            @pl.when(r > 0)
            def _():
                halo_copy(buf, kind, f, 0).wait_send()


def fused(ranks, activation, out_grad, weights, biases):
    height = activation.shape[1]
    extent = activation.shape[2]
    vmem = pltpu.VMEM
    dma = pltpu.SemaphoreType.DMA
    return pl.pallas_call(
        functools.partial(kernel, ranks),
        out_shape=(
            vmem((2, PEERS, 2, OWN, COLS), BF16),
            vmem((ranks, HELD, OWN, CH), BF16),
        ),
        in_specs=[
            pl.BlockSpec(memory_space=pl.ANY),
            pl.BlockSpec(memory_space=pl.ANY),
            pl.BlockSpec(memory_space=pl.ANY),
            pl.BlockSpec(memory_space=pltpu.VMEM),
        ],
        out_specs=[pl.BlockSpec(memory_space=pl.ANY)] * 2,
        scratch_shapes=[
            vmem((OWN, height, extent), BF16),
            vmem((OWN, height, extent), BF16),
            vmem((COLS, COLS), BF16),
            vmem((16, CH, 128), F32),
            vmem((2, PEERS, 2, OWN, COLS), BF16),
            vmem((2, PEERS, 2, OWN, COLS), BF16),
            vmem((2, 4, CH, COLS), BF16),
            vmem((2, 2, CH, COLS), BF16),
            vmem((2, 4, 3 * CH, COLS), BF16),
            vmem((2, 4, CH, COLS), BF16),
            vmem((2, 4, 3 * CH, COLS), BF16),
            vmem((3 * CH, 3 * CH), BF16),
            vmem((3 * CH, 3 * CH), BF16),
            vmem((2, 2, CH, COLS), F32),
            vmem((2, 2, CH, COLS), BF16),
            vmem((3, CH, 3 * CH), F32),
            vmem((CH, 1), F32),
            vmem((PEERS, PIECES, OWN, CH), BF16),
            vmem((ranks // 4 * PEERS, HELD, OWN, CH), BF16),
            vmem((HELD, OWN, CH), BF16),
            pltpu.SemaphoreType.REGULAR((4,)),
            dma((3,)),
            dma((4,)),
            dma((4,)),
            dma((8,)),
            dma((8,)),
            dma((2,)),
            dma((2,)),
            dma,
            dma,
            dma,
            dma,
        ],
        compiler_params=pltpu.CompilerParams(
            collective_id=0, has_side_effects=True, vmem_limit_bytes=60 * 1024 * 1024
        ),
        name="conv_backward",
    )(activation, out_grad, weights, biases)


def outputs_kernel(
    ranks, gin_v, part_v, gin_out, wg_out, bg_out, perm, back, out_v, full, sems
):
    perm[...] = column_phases()
    stores = []
    xs = ranks // 4
    for t in range(PIECES):
        x_of = min(t // HELD, xs - 1)
        at = t - min(HELD * x_of, PIECES - HELD)
        held = [
            part_v[2 * (xs * half + x_of) + core, at].astype(F32)
            for half in range(2)
            for core in range(2)
        ]
        total = (held[0] + held[1]) + (held[2] + held[3])
        if t < 9:
            full[t] = total
        else:
            diagonal = lax.broadcasted_iota(jnp.int32, (OWN, CH), 0) == lax.broadcasted_iota(
                jnp.int32, (OWN, CH), 1
            )
            bg_out[...] = jnp.sum(jnp.where(diagonal, total, 0.0), axis=0)[:OWN]
    store = pltpu.make_async_copy(full, wg_out, sems.at[4])
    store.start()
    stores.append(store)
    for b in range(4):
        cols = slice(128 * b, 128 * (b + 1))
        x = jnp.concatenate(
            [
                jnp.concatenate(
                    [gin_v[h % 2, 2 * phase + (h % 4) // 2, h // 4, :, cols] for phase in range(4)],
                    axis=1,
                )
                for h in range(8)
            ],
            axis=0,
        )
        y = lax.dot_general(x, perm[...], (((1,), (1,)), ((), ())), preferred_element_type=F32)
        for n in range(4):
            back[4 * b + n] = y[:, 128 * n : 128 * (n + 1)]
        for n in range(4):
            for ch in range(OWN):
                rows = back[4 * b + n, pl.ds(ch, 8, stride=OWN), :]
                at = COLS * b + 128 * n
                out_v[ch, :, at : at + 128] = rows.astype(BF16)
        part_of = pl.ds(COLS * b, COLS)
        store = pltpu.make_async_copy(
            out_v.at[:, :, part_of], gin_out.at[:, :, part_of], sems.at[b]
        )
        store.start()
        stores.append(store)

    for store in stores:
        store.wait()


def outputs(ranks, gin, parts, height, extent):
    vmem = pltpu.VMEM
    return pl.pallas_call(
        functools.partial(outputs_kernel, ranks),
        out_shape=(
            jax.ShapeDtypeStruct((OWN, height, extent), BF16),
            jax.ShapeDtypeStruct((9, OWN, CH), F32),
            jax.ShapeDtypeStruct((OWN,), F32),
        ),
        in_specs=[pl.BlockSpec(memory_space=vmem)] * 2,
        out_specs=(
            pl.BlockSpec(memory_space=pl.ANY),
            pl.BlockSpec(memory_space=pl.ANY),
            pl.BlockSpec(memory_space=vmem),
        ),
        scratch_shapes=[
            vmem((COLS, COLS), BF16),
            vmem((16, CH, 128), F32),
            vmem((OWN, height, extent), BF16),
            vmem((9, OWN, CH), F32),
            pltpu.SemaphoreType.DMA((5,)),
        ],
        compiler_params=pltpu.CompilerParams(vmem_limit_bytes=16 * 1024 * 1024),
        name="conv_outputs",
    )(gin, parts)


def shards(ranks, activation, out_grad, weights, biases):
    gin, parts = fused(ranks, activation[0], out_grad[0], weights, biases.reshape(1, CH))
    gin, wg, bg = outputs(ranks, gin, parts, activation.shape[2], activation.shape[3])
    return gin[None], wg, bg


def solution(mesh):
    return jax.shard_map(
        functools.partial(shards, mesh.shape["rows"]),
        mesh=mesh,
        in_specs=(P(None, "chan", "rows", None), P(None, "chan", "rows", None), P(), P()),
        out_specs=(P(None, "chan", "rows", None), P(None, "chan", None), P("chan")),
        check_vma=False,
    )
```

```python
import functools

import jax
import jax.numpy as jnp
from jax import lax
from jax.experimental import pallas as pl
from jax.experimental.pallas import tpu as pltpu
from jax.sharding import PartitionSpec as P

MESH = pl.DeviceIdType.MESH
F32 = jnp.float32
BF16 = jnp.bfloat16

CH = 128
OWN = 16
PEERS = 8
COLS = 512
CHAN_STEPS = [(2, 1), (1, 1), (3, 1), (2, 0), (1, 0), (3, 0), (0, 1)]
ROW_STEPS = [(a, b, e) for a in (1, 0) for b in (2, 1, 3, 0) for e in (1, 0)][:-1]
SHARES = 4


def wait_bytes(ref, sem):
    pltpu.make_async_copy(ref, ref, sem).wait()


def remote(src, dst, send_sem, recv_sem, device):
    return pltpu.make_async_remote_copy(
        src_ref=src,
        dst_ref=dst,
        send_sem=send_sem,
        recv_sem=recv_sem,
        device_id=device,
        device_id_type=MESH,
    )


def local(src, dst, sem):
    return pltpu.make_async_copy(src, dst, sem)


def column_phases():
    w = lax.broadcasted_iota(jnp.int32, (COLS, COLS), 0)
    m = lax.broadcasted_iota(jnp.int32, (COLS, COLS), 1)
    return jnp.where(w == 4 * (m & 127) + (m >> 7), 1.0, 0.0).astype(BF16)


def split_phases(b, block, perm, tmp, send):
    x = block[:, :, COLS * b : COLS * (b + 1)].astype(F32).reshape(CH, COLS).astype(BF16)
    y = jnp.dot(x, perm[...], preferred_element_type=F32)
    for phase in range(4):
        tmp[4 * b + phase] = y[:, 128 * phase : 128 * (phase + 1)]
    for phase in range(4):
        for h in range(8):
            f, half, k = h % 2, (h % 4) // 2, h // 4
            rows = tmp[4 * b + phase, pl.ds(h, OWN, stride=8), :]
            send[f, 2 * phase + half, k, :, 128 * b : 128 * (b + 1)] = rows.astype(BF16)


def stack_shifts(src, dst, ahead):
    def body(i, carry):
        at = pl.multiple_of(i * 32, 32)
        x = src[pl.ds(at, 32), :]
        lane = lax.broadcasted_iota(jnp.int32, (32, COLS), 1)
        xf = x.astype(F32)
        later = jnp.where(lane == 0, 0.0, pltpu.roll(xf, 1, 1)).astype(BF16)
        earlier = jnp.where(lane == COLS - 1, 0.0, pltpu.roll(xf, COLS - 1, 1)).astype(BF16)
        first, last = (earlier, later) if ahead else (later, earlier)
        dst[pl.ds(at, 32), :] = first
        dst[pl.ds(at + 128, 32), :] = x
        dst[pl.ds(at + 256, 32), :] = last
        return carry

    lax.fori_loop(0, CH // 32, body, 0, unroll=True)


def kernel(
    ranks,
    act_ref,
    og_ref,
    w_ref,
    bias_ref,
    gin_out,
    part_r,
    act_v,
    og_v,
    bias_v,
    perm,
    tmp,
    act_s,
    og_s,
    act_a,
    og_a,
    act_x,
    delta_a,
    delta_x,
    w_fwd,
    w_bwd,
    total,
    gin_s,
    gin_r,
    back,
    wg_acc,
    b_acc,
    wg_s,
    wg_r,
    b_s,
    b_r,
    part,
    ring_sem,
    load_sem,
    a2a_send,
    a2a_recv,
    halo_send,
    halo_recv,
    ret_send,
    ret_recv,
    wg_send,
    wg_recv,
    b_send,
    b_recv,
    part_send,
    part_recv,
):
    r = lax.axis_index("rows")
    c = lax.axis_index("chan")
    c16 = pl.multiple_of(c * OWN, OWN)
    far = r // (ranks // 2)

    xs = ranks // 4
    x = lax.rem(r // 2, xs)

    def flipped(at):
        return at + 1 - 2 * lax.rem(at, 2)

    def slot_of(at):
        return at + far * (flipped(at) - at)

    dot = functools.partial(jnp.dot, preferred_element_type=F32)

    barrier = pltpu.get_barrier_semaphore()

    def chan_peer(dz, dy):
        return 2 * lax.rem(c // 2 + dz, PEERS // 2) + lax.rem(c + dy, 2)

    chan_peers = [chan_peer(*step) for step in CHAN_STEPS]
    for to in chan_peers:
        pl.semaphore_signal(barrier, inc=1, device_id={"chan": to}, device_id_type=MESH)

    def ring_peer(step):
        to = lax.rem(r + step + ranks, ranks)
        its = to // (ranks // 2)
        cross = far + its - 2 * far * its
        return {"rows": to, "chan": c + cross * (flipped(c) - c)}

    for step in (1, -1):
        pl.semaphore_signal(barrier, inc=1, device_id=ring_peer(step), device_id_type=MESH)

    loads_act = [
        pltpu.make_async_copy(
            act_ref.at[:, :, pl.ds(COLS * b, COLS)],
            act_v.at[:, :, pl.ds(COLS * b, COLS)],
            load_sem.at[b],
        )
        for b in range(4)
    ]
    for load in loads_act:
        load.start()
    load_og = pltpu.make_async_copy(og_ref, og_v, load_sem.at[4])
    load_og.start()

    def tell(n):
        for step in (2**n, -(2**n))[: 1 if 2 ** (n + 1) == ranks else 2]:
            pl.semaphore_signal(
                ring_sem.at[n], inc=1, device_id=ring_peer(step), device_id_type=MESH
            )

    def hear(n):
        pl.semaphore_wait(ring_sem.at[n], 1 if 2 ** (n + 1) == ranks else 2)

    perm[...] = column_phases()
    for b in range(4):
        loads_act[b].wait()
        split_phases(b, act_v, perm, tmp, act_s)

    pl.semaphore_wait(barrier, PEERS - 1 + 2)

    def exchange(kind, f, send, land, rows):
        for to in chan_peers:
            remote(
                send.at[f, slot_of(to)],
                land.at[f, rows, pl.ds(c16, OWN), :],
                a2a_send.at[2 * kind + f],
                a2a_recv.at[2 * kind + f],
                {"chan": to},
            ).start()
        local(
            send.at[f, slot_of(c)], land.at[f, rows, pl.ds(c16, OWN), :], a2a_recv.at[2 * kind + f]
        ).start()

    def halo_copy(buf, kind, f, down):
        at = 2 * (2 * kind + f) + down
        return remote(buf.at[f, 2 if down else 1], buf.at[f, 0 if down else 3], halo_send.at[at], halo_recv.at[at], ring_peer(1 if down else -1))

    def send_halos(buf, kind, f):
        @pl.when(r < ranks - 1)
        def _():
            halo_copy(buf, kind, f, 1).start()

        @pl.when(r > 0)
        def _():
            halo_copy(buf, kind, f, 0).start()

    def wait_halos(buf, kind, f):
        @pl.when(r > 0)
        def _():
            halo_copy(buf, kind, f, 1).wait_recv()

        @pl.when(r == 0)
        def _():
            buf[f, 0] = jnp.zeros((CH, COLS), BF16)

        @pl.when(r < ranks - 1)
        def _():
            halo_copy(buf, kind, f, 0).wait_recv()

        @pl.when(r == ranks - 1)
        def _():
            buf[f, 3] = jnp.zeros((CH, COLS), BF16)

    own = pl.ds(1, 2)
    both = pl.ds(0, 2)
    exchange(0, 0, act_s, act_a, own)
    exchange(0, 1, act_s, act_a, own)
    for p in range(3):
        for q in range(3):
            pltpu.make_async_copy(
                w_ref.at[3 * p + q],
                w_fwd.at[pl.ds(128 * p, 128), pl.ds(128 * q, 128)],
                load_sem.at[5],
            ).start()
    load_bias = pltpu.make_async_copy(bias_ref, bias_v, load_sem.at[6])
    load_bias.start()
    tell(0)
    load_og.wait()
    for b in range(4):
        split_phases(b, og_v, perm, tmp, og_s)
    exchange(1, 0, og_s, og_a, both)
    exchange(1, 1, og_s, og_a, both)

    pltpu.make_async_copy(w_fwd, w_fwd, load_sem.at[5]).wait()
    load_bias.wait()
    for p in range(3):
        for q in range(3):
            at = (pl.ds(128 * p, 128), pl.ds(128 * q, 128))
            w_bwd[at] = w_fwd[at].astype(F32).T.astype(BF16)
    eye = lax.broadcasted_iota(jnp.int32, (CH, CH), 0) == lax.broadcasted_iota(
        jnp.int32, (CH, CH), 1
    )
    bias = jnp.sum(jnp.where(eye, bias_v[...], 0.0), axis=1, keepdims=True)
    hear(0)
    tell(1)
    b_acc[...] = jnp.zeros_like(b_acc)

    def taps_own(w, x, f, order):
        keep, up, down = order
        for n in range(2):
            cols = pl.ds(256 * n, 256)
            first = x[f, 1, :, cols]
            second = x[f, 2, :, cols]
            w_keep = w[128 * keep : 128 * keep + 128, :]
            w_up = w[128 * up : 128 * up + 128, :]
            w_down = w[128 * down : 128 * down + 128, :]
            total[f, 0, :, cols] = dot(w_keep, first) + dot(w_down, second)
            total[f, 1, :, cols] = dot(w_up, first) + dot(w_keep, second)

    def taps_halo(w, x, f, order):
        keep, up, down = order
        for n in range(2):
            cols = pl.ds(256 * n, 256)
            total[f, 0, :, cols] += dot(w[128 * up : 128 * up + 128, :], x[f, 0, :, cols])
            total[f, 1, :, cols] += dot(w[128 * down : 128 * down + 128, :], x[f, 3, :, cols])

    forward = (1, 0, 2)
    backward = (1, 2, 0)

    def start_act(f):
        wait_bytes(act_a.at[f, own], a2a_recv.at[f])
        send_halos(act_a, 0, f)
        for k in (1, 2):
            stack_shifts(act_a.at[f, k], act_x.at[f, k], False)

        taps_own(w_fwd, act_x, f, forward)

    def finish_pre(f):
        wait_halos(act_a, 0, f)
        for k in (0, 3):
            stack_shifts(act_a.at[f, k], act_x.at[f, k], False)
        taps_halo(w_fwd, act_x, f, forward)

    def make_delta(f):
        wait_bytes(og_a.at[f], a2a_recv.at[2 + f])
        for k in range(2):
            for at in range(0, CH, 16):
                rows = slice(at, at + 16)
                pre = total[f, k, rows, :] + bias[rows, :]
                s = jax.nn.sigmoid(pre)
                delta = (og_a[f, k, rows, :].astype(F32) * s * (1.0 + pre * (1.0 - s))).astype(BF16)
                delta_a[f, 1 + k, rows, :] = delta
                b_acc[rows, :] += jnp.sum(delta.astype(F32), axis=1, keepdims=True)
        send_halos(delta_a, 1, f)

    def tap_row_grad(p, f):
        grads = [
            lax.dot_general(
                delta_a[f, 1 + k],
                act_x[f, k + p],
                (((1,), (1,)), ((), ())),
                preferred_element_type=F32,
            )
            for k in range(2)
        ]
        return grads[0] + grads[1]

    def add_weight_grad(f):
        for p in range(3):
            wg_acc[p] = tap_row_grad(p, f)

    def start_input_grad(f):
        for k in (1, 2):
            stack_shifts(delta_a.at[f, k], delta_x.at[f, k], True)
        taps_own(w_bwd, delta_x, f, backward)

    def make_input_grad(f):
        wait_halos(delta_a, 1, f)
        for k in (0, 3):
            stack_shifts(delta_a.at[f, k], delta_x.at[f, k], True)
        taps_halo(w_bwd, delta_x, f, backward)
        for k in range(2):
            gin_s[f, k] = total[f, k].astype(BF16)

        for to in chan_peers:
            remote(
                gin_s.at[f, :, pl.ds(pl.multiple_of(to * OWN, OWN), OWN), :],
                gin_r.at[f, slot_of(c)],
                ret_send.at[f],
                ret_recv.at[f],
                {"chan": to},
            ).start()
        local(
            gin_s.at[f, :, pl.ds(c16, OWN), :], gin_r.at[f, slot_of(c)], ret_recv.at[f]
        ).start()

    sender = x * PEERS + c

    def send_shares(at, send, land, send_sem, recv_sem):
        def share_copy(to):
            return remote(
                send.at[to],
                land.at[sender],
                send_sem,
                recv_sem,
                {"rows": r + 2 * (at - x), "chan": to},
            )

        for to in chan_peers:
            share_copy(to).start()

        @pl.when(x != at)
        def _():
            share_copy(c).start()

        @pl.when(x == at)
        def _():
            local(send.at[c], land.at[sender], recv_sem).start()

    def send_weight_grad(f):
        for d in range(PEERS):
            rows = slice(OWN * d, OWN * (d + 1))
            b_s[d] = jnp.broadcast_to(b_acc[rows, :], (OWN, CH)).astype(BF16)
        for dx in (2, 1, 3, 0):
            p = lax.rem(x + dx, xs)

            @pl.when(p == 3)
            def _():
                send_shares(p, b_s, b_r, b_send, b_recv)

            @pl.when(p < 3)
            def _():
                grad = (wg_acc[p] + tap_row_grad(p, f)).astype(BF16)
                for d in range(PEERS):
                    for q in range(3):
                        wg_s[p, d, q] = grad[OWN * d : OWN * (d + 1), 128 * q : 128 * (q + 1)]
                send_shares(p, wg_s.at[p], wg_r, wg_send, wg_recv)

    share = 2 * far + lax.rem(r, 2)

    def send_part(src, land):
        for dfar, dx, dcore in ROW_STEPS:
            to = 2 * (xs * lax.rem(far + dfar, 2) + lax.rem(x + dx, xs)) + lax.rem(r + dcore, 2)
            remote(src, land, part_send, part_recv, {"rows": to}).start()
        local(src, land, part_recv).start()

    def send_parts():
        @pl.when(x < 3)
        def _():
            wait_bytes(wg_r, wg_recv)
            for q in range(3):
                acc = wg_r[0, q].astype(F32)
                for d in range(1, xs * PEERS):
                    acc += wg_r[d, q].astype(F32)
                part[q] = acc.astype(BF16)
            send_part(part, part_r.at[pl.ds((x * SHARES + share) * 3, 3)])

        @pl.when(x == 3)
        def _():
            wait_bytes(b_r, b_recv)
            acc = b_r[0].astype(F32)
            for d in range(1, xs * PEERS):
                acc += b_r[d].astype(F32)
            part[0] = acc.astype(BF16)
            send_part(part.at[pl.ds(0, 1)], part_r.at[pl.ds(9 * SHARES + share, 1)])

    def wait_parts_sent():
        @pl.when(x < 3)
        def _():
            wait_bytes(wg_r.at[pl.ds(0, 3 * PEERS - 1)], wg_send)
            wait_bytes(b_r.at[pl.ds(0, PEERS)], b_send)
            wait_bytes(wg_r.at[pl.ds(0, ranks - 1)], part_send)

        @pl.when(x == 3)
        def _():
            wait_bytes(wg_r.at[pl.ds(0, 3 * PEERS)], wg_send)
            wait_bytes(b_r.at[pl.ds(0, PEERS - 1)], b_send)
            wait_bytes(b_r.at[pl.ds(0, ranks - 1)], part_send)

    def join_phases(f):
        wait_bytes(gin_r.at[f], ret_recv.at[f])
        for b in range(4):
            cols = slice(128 * b, 128 * (b + 1))
            x = jnp.concatenate(
                [
                    jnp.concatenate([gin_r[f, 2 * phase + half, k, :, cols] for phase in range(4)], axis=1)
                    for k in range(2)
                    for half in range(2)
                ],
                axis=0,
            )
            y = lax.dot_general(x, perm[...], (((1,), (1,)), ((), ())), preferred_element_type=F32)
            for i in range(4):
                h = 2 * i + f
                for n in range(4):
                    back[4 * b + n, OWN * h : OWN * (h + 1), :] = y[
                        OWN * i : OWN * (i + 1), 128 * n : 128 * (n + 1)
                    ]

    def store_input_grad():
        for n in range(16):
            for ch in range(OWN):
                rows = back[n, pl.ds(ch, 8, stride=OWN), :]
                gin_out[ch, :, 128 * n : 128 * (n + 1)] = rows.astype(BF16)

    start_act(0)
    hear(1)
    tell(2)
    start_act(1)
    hear(2)
    tell(3)
    finish_pre(0)
    make_delta(0)
    finish_pre(1)
    add_weight_grad(0)
    start_input_grad(0)
    hear(3)
    make_delta(1)
    send_weight_grad(1)
    make_input_grad(0)
    start_input_grad(1)
    make_input_grad(1)
    send_parts()
    join_phases(0)
    join_phases(1)
    store_input_grad()
    wait_bytes(part_r, part_recv)

    for f in range(2):
        wait_bytes(act_s.at[f, pl.ds(0, PEERS - 1)], a2a_send.at[f])
        wait_bytes(og_s.at[f, pl.ds(0, PEERS - 1)], a2a_send.at[2 + f])
        wait_bytes(gin_r.at[f, pl.ds(0, PEERS - 1)], ret_send.at[f])
    wait_parts_sent()
    for kind, buf in ((0, act_a), (1, delta_a)):
        for f in range(2):

            @pl.when(r < ranks - 1)
            def _():
                halo_copy(buf, kind, f, 1).wait_send()

            @pl.when(r > 0)
            def _():
                halo_copy(buf, kind, f, 0).wait_send()


def fused(ranks, activation, out_grad, weights, biases):
    height = activation.shape[1]
    extent = activation.shape[2]
    vmem = pltpu.VMEM
    dma = pltpu.SemaphoreType.DMA
    return pl.pallas_call(
        functools.partial(kernel, ranks),
        out_shape=(
            vmem((OWN, height, extent), BF16),
            vmem((10 * SHARES, OWN, CH), BF16),
        ),
        in_specs=[
            pl.BlockSpec(memory_space=pl.ANY),
            pl.BlockSpec(memory_space=pl.ANY),
            pl.BlockSpec(memory_space=pl.ANY),
            pl.BlockSpec(memory_space=pl.ANY),
        ],
        out_specs=[
            pl.BlockSpec(memory_space=pltpu.VMEM),
            pl.BlockSpec(memory_space=pl.ANY),
        ],
        scratch_shapes=[
            vmem((OWN, height, extent), BF16),
            vmem((OWN, height, extent), BF16),
            vmem((1, CH), F32),
            vmem((COLS, COLS), BF16),
            vmem((16, CH, 128), F32),
            vmem((2, PEERS, 2, OWN, COLS), BF16),
            vmem((2, PEERS, 2, OWN, COLS), BF16),
            vmem((2, 4, CH, COLS), BF16),
            vmem((2, 2, CH, COLS), BF16),
            vmem((2, 4, 3 * CH, COLS), BF16),
            vmem((2, 4, CH, COLS), BF16),
            vmem((2, 4, 3 * CH, COLS), BF16),
            vmem((3 * CH, 3 * CH), BF16),
            vmem((3 * CH, 3 * CH), BF16),
            vmem((2, 2, CH, COLS), F32),
            vmem((2, 2, CH, COLS), BF16),
            vmem((2, PEERS, 2, OWN, COLS), BF16),
            vmem((16, CH, 128), F32),
            vmem((3, CH, 3 * CH), F32),
            vmem((CH, 1), F32),
            vmem((3, PEERS, 3, OWN, CH), BF16),
            vmem((4 * PEERS, 3, OWN, CH), BF16),
            vmem((PEERS, OWN, CH), BF16),
            vmem((4 * PEERS, OWN, CH), BF16),
            vmem((3, OWN, CH), BF16),
            pltpu.SemaphoreType.REGULAR((4,)),
            dma((7,)),
            dma((4,)),
            dma((4,)),
            dma((8,)),
            dma((8,)),
            dma((2,)),
            dma((2,)),
            dma,
            dma,
            dma,
            dma,
            dma,
            dma,
        ],
        compiler_params=pltpu.CompilerParams(
            collective_id=0, has_side_effects=True, vmem_limit_bytes=60 * 1024 * 1024
        ),
        name="conv_backward",
    )(activation, out_grad, weights, biases)


def outputs_kernel(gin_ref, part_ref, gin_out, wg_out, bg_out, full, bg_v, sems):
    stores = [pltpu.make_async_copy(gin_ref, gin_out, sems.at[0])]
    stores[0].start()

    def total(shares):
        held = [part_ref[at].astype(F32) for at in shares]
        return (held[0] + held[1]) + (held[2] + held[3])

    for p in range(3):
        for q in range(3):
            full[3 * p + q] = total([(p * SHARES + i) * 3 + q for i in range(SHARES)])
    stores.append(pltpu.make_async_copy(full, wg_out, sems.at[1]))
    stores[1].start()
    diagonal = lax.broadcasted_iota(jnp.int32, (OWN, CH), 0) == lax.broadcasted_iota(
        jnp.int32, (OWN, CH), 1
    )
    bias = total([9 * SHARES + i for i in range(SHARES)])
    bg_v[...] = jnp.sum(jnp.where(diagonal, bias, 0.0), axis=0)[:OWN]
    stores.append(pltpu.make_async_copy(bg_v, bg_out, sems.at[2]))
    stores[2].start()
    for store in stores:
        store.wait()


def outputs(gin, parts):
    vmem = pltpu.VMEM
    return pl.pallas_call(
        outputs_kernel,
        out_shape=(
            jax.ShapeDtypeStruct(gin.shape, BF16),
            jax.ShapeDtypeStruct((9, OWN, CH), F32),
            jax.ShapeDtypeStruct((OWN,), F32),
        ),
        in_specs=[pl.BlockSpec(memory_space=vmem)] * 2,
        out_specs=(
            pl.BlockSpec(memory_space=pl.ANY),
            pl.BlockSpec(memory_space=pl.ANY),
            pl.BlockSpec(memory_space=pl.ANY),
        ),
        scratch_shapes=[vmem((9, OWN, CH), F32), vmem((OWN,), F32), pltpu.SemaphoreType.DMA((3,))],
        compiler_params=pltpu.CompilerParams(vmem_limit_bytes=16 * 1024 * 1024),
        name="conv_outputs",
    )(gin, parts)


def shards(ranks, activation, out_grad, weights, biases):
    gin, parts = fused(ranks, activation[0], out_grad[0], weights, biases.reshape(1, CH))
    gin, wg, bg = outputs(gin, parts)
    return gin[None], wg, bg


def solution(mesh):
    return jax.shard_map(
        functools.partial(shards, mesh.shape["rows"]),
        mesh=mesh,
        in_specs=(P(None, "chan", "rows", None), P(None, "chan", "rows", None), P(), P()),
        out_specs=(P(None, "chan", "rows", None), P(None, "chan", None), P("chan")),
        check_vma=False,
    )
```

```python
import functools

import jax
import jax.numpy as jnp
from jax import lax
from jax.experimental import pallas as pl
from jax.experimental.pallas import tpu as pltpu
from jax.sharding import PartitionSpec as P

MESH = pl.DeviceIdType.MESH
F32 = jnp.float32
BF16 = jnp.bfloat16

CH = 128
OWN = 16
PEERS = 8
COLS = 512
CHAN_STEPS = [(2, 1), (1, 1), (3, 1), (2, 0), (1, 0), (3, 0), (0, 1)]
ROW_STEPS = [(a, b, e) for a in (1, 0) for b in (2, 1, 3, 0) for e in (1, 0)][:-1]
SHARES = 2


def wait_bytes(ref, sem):
    pltpu.make_async_copy(ref, ref, sem).wait()


def remote(src, dst, send_sem, recv_sem, device):
    return pltpu.make_async_remote_copy(
        src_ref=src,
        dst_ref=dst,
        send_sem=send_sem,
        recv_sem=recv_sem,
        device_id=device,
        device_id_type=MESH,
    )


def local(src, dst, sem):
    return pltpu.make_async_copy(src, dst, sem)


def column_phases():
    w = lax.broadcasted_iota(jnp.int32, (COLS, COLS), 0)
    m = lax.broadcasted_iota(jnp.int32, (COLS, COLS), 1)
    return jnp.where(w == 4 * (m & 127) + (m >> 7), 1.0, 0.0).astype(BF16)


def split_phases(b, block, perm, tmp, send):
    x = block[:, :, COLS * b : COLS * (b + 1)].astype(F32).reshape(CH, COLS).astype(BF16)
    y = jnp.dot(x, perm[...], preferred_element_type=F32)
    for phase in range(4):
        tmp[4 * b + phase] = y[:, 128 * phase : 128 * (phase + 1)]
    for phase in range(4):
        for h in range(8):
            f, half, k = h % 2, (h % 4) // 2, h // 4
            rows = tmp[4 * b + phase, pl.ds(h, OWN, stride=8), :]
            send[f, 2 * phase + half, k, :, 128 * b : 128 * (b + 1)] = rows.astype(BF16)


def stack_shifts(src, dst, ahead):
    def body(i, carry):
        at = pl.multiple_of(i * 32, 32)
        x = src[pl.ds(at, 32), :]
        lane = lax.broadcasted_iota(jnp.int32, (32, COLS), 1)
        xf = x.astype(F32)
        later = jnp.where(lane == 0, 0.0, pltpu.roll(xf, 1, 1)).astype(BF16)
        earlier = jnp.where(lane == COLS - 1, 0.0, pltpu.roll(xf, COLS - 1, 1)).astype(BF16)
        first, last = (earlier, later) if ahead else (later, earlier)
        dst[pl.ds(at, 32), :] = first
        dst[pl.ds(at + 128, 32), :] = x
        dst[pl.ds(at + 256, 32), :] = last
        return carry

    lax.fori_loop(0, CH // 32, body, 0, unroll=True)


def kernel(
    ranks,
    act_ref,
    og_ref,
    w_ref,
    bias_ref,
    gin_out,
    part_r,
    act_v,
    og_v,
    bias_v,
    perm,
    tmp,
    act_s,
    og_s,
    act_a,
    og_a,
    act_x,
    delta_a,
    delta_x,
    w_fwd,
    w_bwd,
    total,
    gin_s,
    gin_r,
    back,
    wg_acc,
    b_acc,
    wg_s,
    wg_r,
    wg_c,
    wg_t,
    b_s,
    b_r,
    b_c,
    b_t,
    part,
    ring_sem,
    load_sem,
    a2a_send,
    a2a_recv,
    halo_send,
    halo_recv,
    ret_send,
    ret_recv,
    wg_send,
    wg_recv,
    b_send,
    b_recv,
    core_send,
    core_recv,
    part_send,
    part_recv,
):
    r = lax.axis_index("rows")
    c = lax.axis_index("chan")
    c16 = pl.multiple_of(c * OWN, OWN)
    far = r // (ranks // 2)

    xs = ranks // 4
    x = lax.rem(r // 2, xs)

    def flipped(at):
        return at + 1 - 2 * lax.rem(at, 2)

    def slot_of(at):
        return at + far * (flipped(at) - at)

    dot = functools.partial(jnp.dot, preferred_element_type=F32)

    barrier = pltpu.get_barrier_semaphore()

    def chan_peer(dz, dy):
        return 2 * lax.rem(c // 2 + dz, PEERS // 2) + lax.rem(c + dy, 2)

    chan_peers = [chan_peer(*step) for step in CHAN_STEPS]
    for to in chan_peers:
        pl.semaphore_signal(barrier, inc=1, device_id={"chan": to}, device_id_type=MESH)

    def ring_peer(step):
        to = lax.rem(r + step + ranks, ranks)
        its = to // (ranks // 2)
        cross = far + its - 2 * far * its
        return {"rows": to, "chan": c + cross * (flipped(c) - c)}

    for step in (1, -1):
        pl.semaphore_signal(barrier, inc=1, device_id=ring_peer(step), device_id_type=MESH)

    loads_act = [
        pltpu.make_async_copy(
            act_ref.at[:, :, pl.ds(COLS * b, COLS)],
            act_v.at[:, :, pl.ds(COLS * b, COLS)],
            load_sem.at[b],
        )
        for b in range(4)
    ]
    for load in loads_act:
        load.start()
    load_og = pltpu.make_async_copy(og_ref, og_v, load_sem.at[4])
    load_og.start()

    def tell(n):
        for step in (2**n, -(2**n))[: 1 if 2 ** (n + 1) == ranks else 2]:
            pl.semaphore_signal(
                ring_sem.at[n], inc=1, device_id=ring_peer(step), device_id_type=MESH
            )

    def hear(n):
        pl.semaphore_wait(ring_sem.at[n], 1 if 2 ** (n + 1) == ranks else 2)

    perm[...] = column_phases()
    for b in range(4):
        loads_act[b].wait()
        split_phases(b, act_v, perm, tmp, act_s)

    pl.semaphore_wait(barrier, PEERS - 1 + 2)

    def exchange(at, f, send, land, from_k, to_k):
        for to in chan_peers:
            remote(
                send.at[f, slot_of(to), from_k],
                land.at[f, to_k, pl.ds(c16, OWN), :],
                a2a_send.at[at],
                a2a_recv.at[at],
                {"chan": to},
            ).start()
        local(
            send.at[f, slot_of(c), from_k], land.at[f, to_k, pl.ds(c16, OWN), :], a2a_recv.at[at]
        ).start()

    def halo_copy(buf, kind, f, down):
        at = 2 * (2 * kind + f) + down
        return remote(buf.at[f, 2 if down else 1], buf.at[f, 0 if down else 3], halo_send.at[at], halo_recv.at[at], ring_peer(1 if down else -1))

    def send_halos(buf, kind, f):
        @pl.when(r < ranks - 1)
        def _():
            halo_copy(buf, kind, f, 1).start()

        @pl.when(r > 0)
        def _():
            halo_copy(buf, kind, f, 0).start()

    def wait_halos(buf, kind, f):
        @pl.when(r > 0)
        def _():
            halo_copy(buf, kind, f, 1).wait_recv()

        @pl.when(r == 0)
        def _():
            buf[f, 0] = jnp.zeros((CH, COLS), BF16)

        @pl.when(r < ranks - 1)
        def _():
            halo_copy(buf, kind, f, 0).wait_recv()

        @pl.when(r == ranks - 1)
        def _():
            buf[f, 3] = jnp.zeros((CH, COLS), BF16)

    own = pl.ds(1, 2)
    both = pl.ds(0, 2)
    exchange(0, 0, act_s, act_a, both, own)
    exchange(1, 1, act_s, act_a, both, own)
    for p in range(3):
        for q in range(3):
            pltpu.make_async_copy(
                w_ref.at[3 * p + q],
                w_fwd.at[pl.ds(128 * p, 128), pl.ds(128 * q, 128)],
                load_sem.at[5],
            ).start()
    load_bias = pltpu.make_async_copy(bias_ref, bias_v, load_sem.at[6])
    load_bias.start()
    tell(0)
    load_og.wait()
    for b in range(4):
        split_phases(b, og_v, perm, tmp, og_s)
    exchange(2, 0, og_s, og_a, both, both)
    for k in range(2):
        exchange(3 + k, 1, og_s, og_a, pl.ds(k, 1), pl.ds(k, 1))

    pltpu.make_async_copy(w_fwd, w_fwd, load_sem.at[5]).wait()
    load_bias.wait()
    for p in range(3):
        for q in range(3):
            at = (pl.ds(128 * p, 128), pl.ds(128 * q, 128))
            w_bwd[at] = w_fwd[at].astype(F32).T.astype(BF16)
    eye = lax.broadcasted_iota(jnp.int32, (CH, CH), 0) == lax.broadcasted_iota(
        jnp.int32, (CH, CH), 1
    )
    bias = jnp.sum(jnp.where(eye, bias_v[...], 0.0), axis=1, keepdims=True)
    hear(0)
    tell(1)
    b_acc[...] = jnp.zeros_like(b_acc)

    def taps_own(w, x, f, order):
        keep, up, down = order
        for n in range(2):
            cols = pl.ds(256 * n, 256)
            first = x[f, 1, :, cols]
            second = x[f, 2, :, cols]
            w_keep = w[128 * keep : 128 * keep + 128, :]
            w_up = w[128 * up : 128 * up + 128, :]
            w_down = w[128 * down : 128 * down + 128, :]
            total[f, 0, :, cols] = dot(w_keep, first) + dot(w_down, second)
            total[f, 1, :, cols] = dot(w_up, first) + dot(w_keep, second)

    def taps_halo(w, x, f, order):
        keep, up, down = order
        for n in range(2):
            cols = pl.ds(256 * n, 256)
            total[f, 0, :, cols] += dot(w[128 * up : 128 * up + 128, :], x[f, 0, :, cols])
            total[f, 1, :, cols] += dot(w[128 * down : 128 * down + 128, :], x[f, 3, :, cols])

    forward = (1, 0, 2)
    backward = (1, 2, 0)

    def start_act(f):
        wait_bytes(act_a.at[f, own], a2a_recv.at[f])
        send_halos(act_a, 0, f)
        for k in (1, 2):
            stack_shifts(act_a.at[f, k], act_x.at[f, k], False)

        taps_own(w_fwd, act_x, f, forward)

    def finish_pre(f):
        wait_halos(act_a, 0, f)
        for k in (0, 3):
            stack_shifts(act_a.at[f, k], act_x.at[f, k], False)
        taps_halo(w_fwd, act_x, f, forward)

    def make_delta(f, ks):
        for k in ks:
            for at in range(0, CH, 16):
                rows = slice(at, at + 16)
                pre = total[f, k, rows, :] + bias[rows, :]
                s = jax.nn.sigmoid(pre)
                delta = (og_a[f, k, rows, :].astype(F32) * s * (1.0 + pre * (1.0 - s))).astype(BF16)
                delta_a[f, 1 + k, rows, :] = delta
                b_acc[rows, :] += jnp.sum(delta.astype(F32), axis=1, keepdims=True)

    def tap_row_grad(p, f, k):
        return lax.dot_general(
            delta_a[f, 1 + k],
            act_x[f, k + p],
            (((1,), (1,)), ((), ())),
            preferred_element_type=F32,
        )

    def start_input_grad(f):
        for k in (1, 2):
            stack_shifts(delta_a.at[f, k], delta_x.at[f, k], True)
        taps_own(w_bwd, delta_x, f, backward)

    def make_input_grad(f):
        wait_halos(delta_a, 1, f)
        for k in (0, 3):
            stack_shifts(delta_a.at[f, k], delta_x.at[f, k], True)
        taps_halo(w_bwd, delta_x, f, backward)
        for k in range(2):
            gin_s[f, k] = total[f, k].astype(BF16)

    def return_input_grad(f, k):
        for to in chan_peers:
            remote(
                gin_s.at[f, k, pl.ds(pl.multiple_of(to * OWN, OWN), OWN), :],
                gin_r.at[f, slot_of(c), k],
                ret_send.at[f],
                ret_recv.at[f],
                {"chan": to},
            ).start()
        local(
            gin_s.at[f, k, pl.ds(c16, OWN), :], gin_r.at[f, slot_of(c), k], ret_recv.at[f]
        ).start()

    core = lax.rem(r, 2)
    owner = c // 4 == core
    sender = x * PEERS + c
    other_core = {"rows": r + 1 - 2 * core}

    def block_rows(of, j):
        return pl.ds(pl.multiple_of(64 * of + OWN * j, OWN), OWN)

    def spread(rows):
        return jnp.broadcast_to(b_acc[rows, :], (OWN, CH))

    def exchange_cores(f):
        for j in range(4):
            b_s[j] = spread(block_rows(1 - core, j)).astype(BF16)
        remote(b_s, b_c, core_send.at[3], core_recv.at[3], other_core).start()
        for p in range(3):
            wg_acc[p] += tap_row_grad(p, f, 1)
            for j in range(4):
                for q in range(3):
                    cols = slice(128 * q, 128 * (q + 1))
                    wg_s[p, j, q] = wg_acc[p, block_rows(1 - core, j), cols].astype(BF16)
            remote(wg_s.at[p], wg_c.at[p], core_send.at[p], core_recv.at[p], other_core).start()

    def send_share(at, j, src, dst, send_sem, recv_sem, may_stay):
        to = 4 * core + j
        copy = remote(src, dst, send_sem, recv_sem, {"rows": r + 2 * (at - x), "chan": to})
        if may_stay:

            @pl.when(to != c)
            def _():
                copy.start()

            @pl.when(to == c)
            def _():
                local(src, dst, recv_sem).start()
        else:
            copy.start()

    def send_shares():
        for dx in (2, 1, 3, 0):
            p = lax.rem(x + dx, xs)

            @pl.when(p == 3)
            def _():
                wait_bytes(b_c, core_recv.at[3])
                for step in range(4):
                    j = lax.rem(c + 1 + step, 4)
                    b_t[j] = (spread(block_rows(core, j)) + b_c[j].astype(F32)).astype(BF16)
                    send_share(p, j, b_t.at[j], b_r.at[sender], b_send, b_recv, dx == 0 and step == 3)

            @pl.when(p < 3)
            def _():
                wait_bytes(wg_c.at[p], core_recv.at[p])
                for step in range(4):
                    j = lax.rem(c + 1 + step, 4)
                    for q in range(3):
                        mine = wg_acc[p, block_rows(core, j), 128 * q : 128 * (q + 1)]
                        wg_t[p, j, q] = (mine + wg_c[p, j, q].astype(F32)).astype(BF16)
                    send_share(p, j, wg_t.at[p, j], wg_r.at[sender], wg_send, wg_recv, dx == 0 and step == 3)

    def send_part(src, land):
        for dfar, dx, dcore in ROW_STEPS:
            to = 2 * (xs * lax.rem(far + dfar, 2) + lax.rem(x + dx, xs)) + lax.rem(r + dcore, 2)
            remote(src, land, part_send, part_recv, {"rows": to}).start()
        local(src, land, part_recv).start()

    taps_owner = jnp.logical_and(owner, x < 3)
    bias_owner = jnp.logical_and(owner, x == 3)

    def send_parts():
        @pl.when(taps_owner)
        def _():
            wait_bytes(wg_r, wg_recv)
            for q in range(3):
                acc = wg_r[0, q].astype(F32)
                for d in range(1, 4 * PEERS):
                    acc += wg_r[d, q].astype(F32)
                part[q] = acc.astype(BF16)
            send_part(part, part_r.at[pl.ds((x * SHARES + far) * 3, 3)])

        @pl.when(bias_owner)
        def _():
            wait_bytes(b_r, b_recv)
            acc = b_r[0].astype(F32)
            for d in range(1, 4 * PEERS):
                acc += b_r[d].astype(F32)
            part[0] = acc.astype(BF16)
            send_part(part.at[pl.ds(0, 1)], part_r.at[pl.ds(9 * SHARES + far, 1)])

    def wait_parts_sent():
        for p in range(3):
            wait_bytes(wg_s.at[p], core_send.at[p])
        wait_bytes(b_s, core_send.at[3])

        @pl.when(taps_owner)
        def _():
            wait_bytes(wg_r.at[pl.ds(0, 11)], wg_send)
            wait_bytes(wg_r.at[pl.ds(0, ranks - 1)], part_send)

        @pl.when(jnp.logical_not(taps_owner))
        def _():
            wait_bytes(wg_r.at[pl.ds(0, 12)], wg_send)

        @pl.when(bias_owner)
        def _():
            wait_bytes(b_r.at[pl.ds(0, 3)], b_send)
            wait_bytes(b_r.at[pl.ds(0, ranks - 1)], part_send)

        @pl.when(jnp.logical_not(bias_owner))
        def _():
            wait_bytes(b_r.at[pl.ds(0, 4)], b_send)

    def join_phases(f):
        wait_bytes(gin_r.at[f], ret_recv.at[f])
        for b in range(4):
            cols = slice(128 * b, 128 * (b + 1))
            x = jnp.concatenate(
                [
                    jnp.concatenate([gin_r[f, 2 * phase + half, k, :, cols] for phase in range(4)], axis=1)
                    for k in range(2)
                    for half in range(2)
                ],
                axis=0,
            )
            y = lax.dot_general(x, perm[...], (((1,), (1,)), ((), ())), preferred_element_type=F32)
            for i in range(4):
                h = 2 * i + f
                for n in range(4):
                    back[4 * b + n, OWN * h : OWN * (h + 1), :] = y[
                        OWN * i : OWN * (i + 1), 128 * n : 128 * (n + 1)
                    ]

    def store_input_grad():
        for n in range(16):
            for ch in range(OWN):
                rows = back[n, pl.ds(ch, 8, stride=OWN), :]
                gin_out[ch, :, 128 * n : 128 * (n + 1)] = rows.astype(BF16)

    start_act(0)
    hear(1)
    tell(2)
    start_act(1)
    hear(2)
    tell(3)
    finish_pre(0)
    wait_bytes(og_a.at[0], a2a_recv.at[2])
    make_delta(0, (0, 1))
    send_halos(delta_a, 1, 0)
    finish_pre(1)
    for p in range(3):
        wg_acc[p] = tap_row_grad(p, 0, 0) + tap_row_grad(p, 0, 1)
    start_input_grad(0)
    hear(3)
    wait_bytes(og_a.at[1, pl.ds(0, 1)], a2a_recv.at[3])
    make_delta(1, (0,))
    for p in range(3):
        wg_acc[p] += tap_row_grad(p, 1, 0)
    wait_bytes(og_a.at[1, pl.ds(1, 1)], a2a_recv.at[4])
    make_delta(1, (1,))
    send_halos(delta_a, 1, 1)
    exchange_cores(1)
    make_input_grad(0)
    send_shares()
    return_input_grad(0, 0)
    return_input_grad(0, 1)
    start_input_grad(1)
    make_input_grad(1)
    return_input_grad(1, 0)
    send_parts()
    return_input_grad(1, 1)
    join_phases(0)
    join_phases(1)
    store_input_grad()
    wait_bytes(part_r, part_recv)

    wait_bytes(og_s.at[0, pl.ds(0, PEERS - 1)], a2a_send.at[2])
    for f in range(2):
        wait_bytes(act_s.at[f, pl.ds(0, PEERS - 1)], a2a_send.at[f])
        wait_bytes(og_s.at[1, pl.ds(0, PEERS - 1), pl.ds(f, 1)], a2a_send.at[3 + f])
        wait_bytes(gin_r.at[f, pl.ds(0, PEERS - 1)], ret_send.at[f])
    wait_parts_sent()
    for kind, buf in ((0, act_a), (1, delta_a)):
        for f in range(2):

            @pl.when(r < ranks - 1)
            def _():
                halo_copy(buf, kind, f, 1).wait_send()

            @pl.when(r > 0)
            def _():
                halo_copy(buf, kind, f, 0).wait_send()


def fused(ranks, activation, out_grad, weights, biases):
    height = activation.shape[1]
    extent = activation.shape[2]
    vmem = pltpu.VMEM
    dma = pltpu.SemaphoreType.DMA
    return pl.pallas_call(
        functools.partial(kernel, ranks),
        out_shape=(
            vmem((OWN, height, extent), BF16),
            vmem((10 * SHARES, OWN, CH), BF16),
        ),
        in_specs=[
            pl.BlockSpec(memory_space=pl.ANY),
            pl.BlockSpec(memory_space=pl.ANY),
            pl.BlockSpec(memory_space=pl.ANY),
            pl.BlockSpec(memory_space=pl.ANY),
        ],
        out_specs=[
            pl.BlockSpec(memory_space=pltpu.VMEM),
            pl.BlockSpec(memory_space=pl.ANY),
        ],
        scratch_shapes=[
            vmem((OWN, height, extent), BF16),
            vmem((OWN, height, extent), BF16),
            vmem((1, CH), F32),
            vmem((COLS, COLS), BF16),
            vmem((16, CH, 128), F32),
            vmem((2, PEERS, 2, OWN, COLS), BF16),
            vmem((2, PEERS, 2, OWN, COLS), BF16),
            vmem((2, 4, CH, COLS), BF16),
            vmem((2, 2, CH, COLS), BF16),
            vmem((2, 4, 3 * CH, COLS), BF16),
            vmem((2, 4, CH, COLS), BF16),
            vmem((2, 4, 3 * CH, COLS), BF16),
            vmem((3 * CH, 3 * CH), BF16),
            vmem((3 * CH, 3 * CH), BF16),
            vmem((2, 2, CH, COLS), F32),
            vmem((2, 2, CH, COLS), BF16),
            vmem((2, PEERS, 2, OWN, COLS), BF16),
            vmem((16, CH, 128), F32),
            vmem((3, CH, 3 * CH), F32),
            vmem((CH, 1), F32),
            vmem((3, 4, 3, OWN, CH), BF16),
            vmem((4 * PEERS, 3, OWN, CH), BF16),
            vmem((3, 4, 3, OWN, CH), BF16),
            vmem((3, 4, 3, OWN, CH), BF16),
            vmem((4, OWN, CH), BF16),
            vmem((4 * PEERS, OWN, CH), BF16),
            vmem((4, OWN, CH), BF16),
            vmem((4, OWN, CH), BF16),
            vmem((3, OWN, CH), BF16),
            pltpu.SemaphoreType.REGULAR((4,)),
            dma((7,)),
            dma((5,)),
            dma((5,)),
            dma((8,)),
            dma((8,)),
            dma((2,)),
            dma((2,)),
            dma,
            dma,
            dma,
            dma,
            dma((4,)),
            dma((4,)),
            dma,
            dma,
        ],
        compiler_params=pltpu.CompilerParams(
            collective_id=0, has_side_effects=True, vmem_limit_bytes=60 * 1024 * 1024
        ),
        name="conv_backward",
    )(activation, out_grad, weights, biases)


def outputs_kernel(gin_ref, part_ref, gin_out, wg_out, bg_out, full, bg_v, sems):
    stores = [pltpu.make_async_copy(gin_ref, gin_out, sems.at[0])]
    stores[0].start()

    def total(shares):
        held = [part_ref[at].astype(F32) for at in shares]
        return held[0] + held[1]

    for p in range(3):
        for q in range(3):
            full[3 * p + q] = total([(p * SHARES + i) * 3 + q for i in range(SHARES)])
    stores.append(pltpu.make_async_copy(full, wg_out, sems.at[1]))
    stores[1].start()
    diagonal = lax.broadcasted_iota(jnp.int32, (OWN, CH), 0) == lax.broadcasted_iota(
        jnp.int32, (OWN, CH), 1
    )
    bias = total([9 * SHARES + i for i in range(SHARES)])
    bg_v[...] = jnp.sum(jnp.where(diagonal, bias, 0.0), axis=0)[:OWN]
    stores.append(pltpu.make_async_copy(bg_v, bg_out, sems.at[2]))
    stores[2].start()
    for store in stores:
        store.wait()


def outputs(gin, parts):
    vmem = pltpu.VMEM
    return pl.pallas_call(
        outputs_kernel,
        out_shape=(
            jax.ShapeDtypeStruct(gin.shape, BF16),
            jax.ShapeDtypeStruct((9, OWN, CH), F32),
            jax.ShapeDtypeStruct((OWN,), F32),
        ),
        in_specs=[pl.BlockSpec(memory_space=vmem)] * 2,
        out_specs=(
            pl.BlockSpec(memory_space=pl.ANY),
            pl.BlockSpec(memory_space=pl.ANY),
            pl.BlockSpec(memory_space=pl.ANY),
        ),
        scratch_shapes=[vmem((9, OWN, CH), F32), vmem((OWN,), F32), pltpu.SemaphoreType.DMA((3,))],
        compiler_params=pltpu.CompilerParams(vmem_limit_bytes=16 * 1024 * 1024),
        name="conv_outputs",
    )(gin, parts)


def shards(ranks, activation, out_grad, weights, biases):
    gin, parts = fused(ranks, activation[0], out_grad[0], weights, biases.reshape(1, CH))
    gin, wg, bg = outputs(gin, parts)
    return gin[None], wg, bg


def solution(mesh):
    return jax.shard_map(
        functools.partial(shards, mesh.shape["rows"]),
        mesh=mesh,
        in_specs=(P(None, "chan", "rows", None), P(None, "chan", "rows", None), P(), P()),
        out_specs=(P(None, "chan", "rows", None), P(None, "chan", None), P("chan")),
        check_vma=False,
    )
```
